512 devices in a mesh: cuts: 32 (over y, x_hi, core), mode: 16 (over x_lo, z).
Axes of the slice: x: 4 (x_hi: 2, x_lo: 2; x = x_hi * 2 + x_lo), y: 8, z: 8, core: 2. Of those that a mesh axis runs over, the one named last changes fastest.
Arguments:
- stem: float32 [32, 16, 16, 32768], P('cuts', 'mode'), may hold values from -1.5 to 1.5
- left: float32 [6, 2, 512, 512], P(None, None, 'mode'), may hold values from -0.25 to 0.25
- right: float32 [512, 512], replicated, may hold values from -0.25 to 0.25
- slice_bits: int32 [32, 6], P('cuts'), may hold values from 0 to 1
- leg_order: int32 [6, 9], replicated, may hold values from 0 to 8, each once within a row
Outputs:
- amplitudes: float32 [16, 16, 32768], P(None, 'mode', 'cuts')
The draws below stay inside these ranges and needn't reach their ends.
Inputs may be any that keep to these rules, and one draw needn't show every extreme that they name: slice_bits[s, t] is the value of branch t's cut bond in slice s. Each row of leg_order is a permutation of 0 to 8.
All inputs are finite; a program needn't handle non-finite values.
Results may differ from the reference program's by a relative error of at most 0.00018.
Values sent between devices are 32-bit elements; how exact they have to be, the bound alone decides.
A program may use at most 64 MiB of HBM per device.

```python
import jax
import jax.numpy as jnp
from jax import lax

LEGS = 9
BRANCH = 512
TAIL_MODES = 15
TAIL = 32768
HEAD = 16
BRANCHES = 6
SLICES = 32


def touch_ends(values, rng, low, largest):
    shape = values.shape
    place = [jax.random.randint(jax.random.fold_in(rng, axis), (), 0, shape[axis]) for axis in range(len(shape))]
    values = values.at[tuple(place)].set(low)
    longest = shape.index(max(shape))
    place[longest] = (place[longest] + 1) % shape[longest]
    return values.at[tuple(place)].set(largest)


def shard_levels(own_key, extent, pieces, least, largest):
    def one(axis_at, parts):
        steps = jax.random.uniform(jax.random.fold_in(jax.random.fold_in(own_key, 6), axis_at), (parts,), jnp.float32, least / len(pieces), largest / len(pieces))
        return jnp.repeat(jnp.exp(steps), extent[axis_at] // parts).reshape((-1,) + (1,) * (len(extent) - axis_at - 1))

    level = one(*pieces[0])
    for cut in pieces[1:]:
        level = level * one(*cut)
    return level


def scatter_about(rng, shape, scale, limit, shards=(), held_as=jnp.bfloat16):
    factor_of = shard_levels(rng, shape, shards, -0.22, 0.18) if shards else 1.0
    values = jax.random.normal(rng, shape, jnp.float32) * scale * factor_of
    return jnp.minimum(jnp.maximum(values, -limit), limit).astype(held_as)


def setup_inputs(seed: int = 0) -> dict:
    streams_of = jax.random.split(jax.random.key(seed), 6)
    return {
        "stem": scatter_about(streams_of[0], (SLICES, HEAD, HEAD, TAIL), 0.25, 1.5, ((0, 32), (1, 16)), jnp.float32),
        "left": scatter_about(streams_of[1], (BRANCHES, 2, BRANCH, BRANCH), BRANCH ** -0.5, 0.25, ((2, 16),), jnp.float32),
        "right": scatter_about(streams_of[2], (BRANCH, BRANCH), BRANCH ** -0.5, 0.25, (), jnp.float32),
        "slice_bits": touch_ends(jax.random.randint(streams_of[3], (SLICES, BRANCHES), 0, 2), jax.random.fold_in(streams_of[3], 1), 0, 1).astype(jnp.int32),
        "leg_order": jax.vmap(lambda own: jax.random.permutation(own, LEGS))(jax.random.split(streams_of[4], BRANCHES)).reshape((BRANCHES, LEGS)).astype(jnp.int32),
    }


HIGHEST_PRECISION = lax.Precision.HIGHEST


def leg_columns(leg_map, leg_count):
    indices = jnp.arange(2 ** leg_count, dtype=jnp.int32)
    shifts = (leg_count - 1 - leg_map).astype(jnp.int32)
    chosen = jnp.right_shift(indices[:, None], shifts[None, :]) & 1
    powers = jnp.left_shift(jnp.ones((leg_count,), jnp.int32), (leg_count - 1 - jnp.arange(leg_count, dtype=jnp.int32)))
    return jnp.sum(chosen * powers[None, :], axis=1).astype(jnp.int32)


def run_absorb(tensor, matrix, first, leg_count):
    branch_size = 2 ** leg_count
    after = tensor.size // (2 ** first * branch_size)
    shaped = tensor.reshape(2 ** first, branch_size, after)
    result = jnp.einsum("ji,pir->pjr", matrix, shaped, precision=HIGHEST_PRECISION)
    return result.reshape(tensor.shape)


def head_absorb(tensor, matrix, leg_count):
    inner = 2 ** (leg_count - 4)
    shaped = tensor.reshape(16, 16, inner, -1)
    blocks = matrix.reshape(16, inner, 16, inner)
    result = jnp.einsum("abcd,cxdr->axbr", blocks, shaped, precision=HIGHEST_PRECISION)
    return result.reshape(tensor.shape)


def pair_absorb(tensor, matrix, leg_count):
    inner = 2 ** (leg_count - 2)
    shaped = tensor.reshape(4, 4, 16, inner, -1)
    blocks = matrix.reshape(4, inner, 4, inner)
    result = jnp.einsum("bdce,acxer->abxdr", blocks, shaped, precision=HIGHEST_PRECISION)
    return result.reshape(tensor.shape)


def reference(stem, left, right, slice_bits, leg_order):
    total_modes = 8 + TAIL_MODES
    permuted = [jnp.take(right, leg_columns(leg_order[branch], LEGS), axis=1) for branch in range(6)]

    def one_slice(summed, inputs):
        tensor, bits = inputs
        matrices = [jnp.dot(left[branch][bits[branch]], permuted[branch], precision=HIGHEST_PRECISION) for branch in range(6)]
        tensor = run_absorb(tensor, matrices[0], total_modes - LEGS, LEGS)
        tensor = run_absorb(tensor, matrices[1], 6, LEGS)
        tensor = run_absorb(tensor, matrices[2], 4, LEGS)
        tensor = head_absorb(tensor, matrices[3], LEGS)
        tensor = run_absorb(tensor, matrices[4], total_modes - LEGS, LEGS)
        tensor = pair_absorb(tensor, matrices[5], LEGS)
        return summed + tensor, None

    summed, unused = lax.scan(one_slice, jnp.zeros(stem.shape[1:], stem.dtype), (stem, slice_bits))
    return summed
```

```python
import functools

import jax
import jax.numpy as jnp
from jax import lax
from jax.experimental import pallas as pl
from jax.experimental.pallas import tpu as pltpu
from jax.sharding import PartitionSpec as P

F32, BF16, I32 = jnp.float32, jnp.bfloat16, jnp.int32
MESH = pl.DeviceIdType.MESH
LINE = (0, 2)
RING = (1, 4, 3, 5)
NATURAL9 = (0, 1, 2, 3, 4, 5, 6, 7, 8)
COLUMNS = {1: (8, 0, 1, 2, 3, 4, 5, 6, 7), 5: (7, 8, 0, 1, 2, 3, 4, 5, 6)}
ROWS = {1: (3, 4, 0, 1, 2), 5: (2, 1, 0, 3, 4)}


def halves(a):
    high = a.astype(BF16)
    return high, (a - high.astype(F32)).astype(BF16)


def dot(a, b, transposed=False):
    dims = (((1,), (1 if transposed else 0,)), ((), ()))
    return lax.dot_general(a, b, dims, preferred_element_type=F32)


def dot3(a, b, transposed=False):
    (ah, al), (bh, bl) = a, b
    return dot(ah, bl, transposed) + dot(al, bh, transposed) + dot(ah, bh, transposed)


def reordered(index, order):
    bits = len(order)
    total = jnp.zeros_like(index)
    for place, leg in enumerate(order):
        bit = jnp.right_shift(index, bits - 1 - place) & 1
        total = total + jnp.left_shift(bit, bits - 1 - leg)
    return total


def one_hot(rows, columns):
    return jnp.where(rows == columns, 1.0, 0.0).astype(BF16)


def fragments(order, bits, left, right, fz, fy, sel):
    product = dot3(halves(left[...].reshape(384, 512)), halves(right[...]))
    for t in range(6):
        part = product[64 * t : 64 * t + 64]
        first = part.astype(BF16)
        rest = part - first.astype(F32)
        second = rest.astype(BF16)
        third = (rest - second.astype(F32)).astype(BF16)
        stacked = jnp.concatenate([first, second, third], axis=0)
        spot = lax.broadcasted_iota(I32, (8, 512), 1)
        spot = reordered(spot, COLUMNS.get(t, NATURAL9))
        column = jnp.zeros_like(spot)
        for q in range(9):
            bit = jnp.right_shift(spot, jnp.full_like(spot, 8 - order[t, q])) & 1
            column = column + jnp.left_shift(bit, 8 - q)
        moved = dot(stacked, one_hot(lax.broadcasted_iota(I32, (512, 512), 0), column[0:1]))
        pieces = [moved[64 * k : 64 * k + 64] for k in range(3)]
        if t in ROWS:
            new = lax.broadcasted_iota(I32, (64, 64), 0)
            old = (new & 32) + reordered(new & 31, ROWS[t])
            turn = one_hot(lax.broadcasted_iota(I32, (64, 64), 1), old)
            pieces = [dot(turn, p.astype(BF16)) for p in pieces]
        value = pieces[0] + pieces[1] + pieces[2]
        mine = jnp.full((8, 256), bits[0, t], I32)
        if t in LINE:
            wide = jnp.full((32, 512), bits[0, t], I32)
            fz[LINE.index(t)] = jnp.where(wide == 1, value[32:], value[:32])
        else:
            k = RING.index(t)
            sel[k] = mine
            for s in range(8):
                for h in range(2):
                    fy[k, s, h] = value[8 * s : 8 * s + 8, 256 * h : 256 * h + 256]


def contract(
    stem, fz, fy, sel, out,
    gz, gy, bh, bl, y0, y1, w, tt, rr, s3, acc, twin, part, final, last,
    z_send, z_recv, x_send, x_recv, base_send, base_recv, y_send, y_recv, d_send, d_recv,
    a_send, a_recv, t_send, t_recv, r_send, r_recv, l_send, l_recv,
):
    c, m = lax.axis_index("cuts"), lax.axis_index("mode")
    xl, z = m // 8, lax.rem(m, 8)
    y, xh, core = c // 4, lax.rem(c // 2, 2), lax.rem(c, 2)
    z_next = [(c, xl * 8 + lax.rem(z + 1, 8)), (c, xl * 8 + lax.rem(z + 7, 8))]
    y_next = [(lax.rem(y + 1, 8) * 4 + lax.rem(c, 4), m), (lax.rem(y + 7, 8) * 4 + lax.rem(c, 4), m)]
    sibling = (c + 1 - 2 * core, m)
    across = (c + 2 - 4 * xh, m)
    beside = (c, m + 8 - 16 * xl)

    def peer(k):
        return lax.rem(m + k, 16)

    barrier = pltpu.get_barrier_semaphore()

    @pl.loop(1, 16)
    def _(k):
        pl.semaphore_signal(barrier, inc=1, device_id=(c, peer(k)), device_id_type=MESH)

    for target in (*y_next, sibling, across):
        pl.semaphore_signal(barrier, inc=1, device_id=target, device_id_type=MESH)
    for k in range(2):
        gz[k, m] = fz[k]
    for t in range(4):
        gy[t, y, core, m] = fy[t, y, core]
    pl.semaphore_wait(barrier, 19)

    started = []

    def remote(src, dst, send, recv, target):
        return pltpu.make_async_remote_copy(
            src_ref=src, dst_ref=dst, send_sem=send, recv_sem=recv, device_id=target, device_id_type=MESH
        )

    def go(copy):
        copy.start()
        started.append(copy)

    def x_copy(k):
        return remote(gz.at[k, m], gz.at[k, m], x_send.at[k], x_recv.at[k], beside)

    def z_copy(k, cls, d, s):
        owner = lax.rem(z + 8 - (1 - 2 * d) * (s - 1), 8)
        row = (xl * 8 if cls == 0 else (1 - xl) * 8) + owner
        piece = gz.at[k, row]
        if s == 4:
            piece = gz.at[k, row, pl.ds(16 * d, 16)]
        return remote(piece, piece, z_send.at[k, cls, d, s - 1], z_recv.at[k, cls, d, s - 1], z_next[d])

    def z_step(k, s):
        for cls in range(2):
            if s == 1 and cls == 1:
                x_copy(k).wait_recv()
            for d in range(2):
                if s > 1:
                    z_copy(k, cls, d, s - 1).wait_recv()
                go(z_copy(k, cls, d, s))

    def z_finish(k):
        for cls in range(2):
            for d in range(2):
                z_copy(k, cls, d, 4).wait_recv()

    def base_copy(g, k):
        pair = pl.ds(2 * g, 2)
        return remote(
            fy.at[pair, y, core], gy.at[pair, y, core, m],
            base_send.at[g, k], base_recv.at[g, k], (c, peer(k)),
        )

    def base_start(g):
        @pl.loop(1, 16)
        def _(k):
            base_copy(g, k).start()

    def base_wait(g):
        @pl.loop(1, 16)
        def _(k):
            base_copy(g, k).wait_recv()

    def y_copy(t, d, s):
        owner = lax.rem(y + 8 - (1 - 2 * d) * (s - 1), 8)
        piece = gy.at[t, owner, core]
        if s == 4:
            piece = gy.at[t, owner, core, pl.ds(8 * d, 8)]
        return remote(piece, piece, y_send.at[t, d, s - 1], y_recv.at[t, d, s - 1], y_next[d])

    def d_copy(t, n):
        if n == 0:
            slot = y
        elif n == 7:
            slot = lax.rem(y + 4, 8)
        else:
            slot = lax.rem(y + 8 - (1 - 2 * ((n - 1) % 2)) * ((n + 1) // 2), 8)
        piece = gy.at[t, slot, core]
        return remote(piece, piece, d_send.at[t, n], d_recv.at[t, n], sibling)

    def y_step(t, s):
        if s == 1:
            if t % 2 == 0:
                base_wait(t // 2)
            for d in range(2):
                go(y_copy(t, d, 1))
            go(d_copy(t, 0))
            return
        for d in range(2):
            y_copy(t, d, s - 1).wait_recv()
            if s < 5:
                go(y_copy(t, d, s))
                go(d_copy(t, 2 * (s - 1) - 1 + d))
        if s == 5:
            go(d_copy(t, 7))

    def y_finish(t):
        for n in range(8):
            d_copy(t, n).wait_recv()

    def prepare_line(k):
        b = LINE[k]

        @pl.loop(0, 4)
        def _(i):
            rows = pl.ds(pl.multiple_of(128 * i, 128), 128)
            bh[b, rows], bl[b, rows] = halves(gz[k, pl.ds(4 * i, 4)].reshape(128, 512))

    def prepare_ring(t):
        b = RING[t]
        one = sel[t] == 1

        @pl.loop(0, 16)
        def _(i):
            rows = pl.ds(pl.multiple_of(32 * i, 32), 32)
            for h in range(2):
                lanes = slice(256 * h, 256 * h + 256)
                value = jnp.concatenate(
                    [jnp.where(one, gy[t, 4 + q, h, i], gy[t, q, h, i]) for q in range(4)], axis=0
                )
                bh[b, rows, lanes], bl[b, rows, lanes] = halves(value)

    def prepare_turned(t, turn=None):
        b = RING[t]
        one = (sel[t] == 1)[None]

        @pl.loop(0, 4)
        def _(q):
            rows = pl.ds(pl.multiple_of(128 * q, 128), 128)
            for h in range(2):
                lanes = slice(256 * h, 256 * h + 256)
                value = jnp.where(one, gy[t, 4 + q, h], gy[t, q, h]).reshape(128, 256)
                high, low = halves(value)
                if turn is not None:
                    high, low = dot(turn, high).astype(BF16), dot(turn, low).astype(BF16)
                bh[b, rows, lanes], bl[b, rows, lanes] = high, low

    def matrix(b):
        return bh[b], bl[b]

    def absorb0():
        @pl.loop(0, 2)
        def _(i):
            rows = pl.ds(pl.multiple_of(512 * i, 512), 512)
            y0[rows] = dot3(halves(stem[rows]), matrix(0), True)

    def absorb1():
        @pl.loop(0, 4)
        def _(i):
            rows = pl.ds(pl.multiple_of(256 * i, 256), 256)
            data = jnp.concatenate([y0[rows, :256], y0[rows, 256:]], axis=0)
            new = dot3(matrix(1), halves(data))
            for m13 in range(2):
                for h in range(2):
                    at = 128 * (2 * m13 + h)
                    y1[h, i, m13] = new[at : at + 128]

    def absorb4():
        @pl.loop(0, 2)
        def _(i):
            pair = pl.ds(2 * i, 2)
            data = jnp.concatenate([y1[0, pair].reshape(512, 256), y1[1, pair].reshape(512, 256)], axis=1)
            new = dot3(halves(data), matrix(4), True)
            for k in range(2):
                for m13 in range(2):
                    for h in range(2):
                        at = 128 * (2 * k + m13)
                        w[2 * m13 + h, 2 * i + k] = new[at : at + 128, 256 * h : 256 * h + 256]

    def a_copy(q, k):
        return remote(
            tt.at[q, peer(k)], rr.at[q, m], a_send.at[q, k], a_recv.at[q, k], (c, peer(k))
        )

    def absorb2():
        @pl.loop(0, 4)
        def _(q):
            new = dot3(matrix(2), halves(w[q].reshape(512, 256)))
            tt[q] = new.reshape(16, 32, 256)
            rr[q, m] = tt[q, m]

            @pl.loop(1, 16)
            def _(k):
                a_copy(q, k).start()

    def absorb3():
        @pl.loop(0, 4)
        def _(q):
            @pl.loop(1, 16)
            def _(k):
                a_copy(q, k).wait_recv()

            new = dot3(matrix(3), halves(rr[q].reshape(512, 256)))
            s3[q] = new.reshape(4, 128, 256)

    def t_copy(i):
        return remote(acc.at[1 - core, i], twin.at[i], t_send.at[i], t_recv.at[i], sibling)

    def absorb5(half, send):
        rows = pl.ds(pl.multiple_of(256 * half, 256), 256)

        @pl.loop(0, 4)
        def _(i):
            data = s3[:, i].reshape(512, 256)
            new = dot3((bh[5, rows], bl[5, rows]), halves(data)).reshape(2, 8, 16, 256)
            if send:
                acc[half, i] = new
                t_copy(i).start()
            else:
                t_copy(i).wait_recv()
                acc[half, i] = new + twin[i]

    def steps(k, d):
        return 4 if k == d else 3

    def r_copy(k, d, s):
        n = steps(k, d)
        dest = lax.rem(y + 8 + (1 - 2 * d) * (n - s + 1), 8)
        src = acc.at[core, :, k, dest] if s == 1 else part.at[k, d, s - 2]
        return remote(src, part.at[k, d, s - 1], r_send.at[k, d, s - 1], r_recv.at[k, d, s - 1], y_next[d])

    def reduce():
        order = [(k, d) for d in range(2) for k in range(2)]
        for k, d in order:
            go(r_copy(k, d, 1))
        for s in range(2, 5):
            for k, d in order:
                n = steps(k, d)
                if s <= n:
                    dest = lax.rem(y + 8 + (1 - 2 * d) * (n - s + 1), 8)
                    r_copy(k, d, s - 1).wait_recv()
                    part[k, d, s - 2] = part[k, d, s - 2] + acc[core, :, k, dest]
                    go(r_copy(k, d, s))
        for k in range(2):
            for d in range(2):
                r_copy(k, d, steps(k, d)).wait_recv()
            final[k] = acc[core, :, k, y] + part[k, 0, steps(k, 0) - 1] + part[k, 1, steps(k, 1) - 1]
        swap = remote(final.at[1 - xh], last, l_send, l_recv, across)
        go(swap)
        swap.wait_recv()
        out[...] = (final[xh] + last[...]).reshape(64, 256)

    go(x_copy(0))
    base_start(0)
    z_step(0, 1)
    z_step(0, 2)
    y_step(0, 1)
    go(x_copy(1))
    z_step(1, 1)
    z_step(0, 3)
    y_step(0, 2)
    y_step(1, 1)
    base_start(1)
    z_step(1, 2)
    z_step(0, 4)
    y_step(0, 3)
    y_step(1, 2)
    z_step(1, 3)
    z_finish(0)
    y_step(0, 4)
    y_step(1, 3)
    z_step(1, 4)
    prepare_line(0)
    absorb0()
    y_step(0, 5)
    y_step(1, 4)
    y_step(2, 1)
    y_finish(0)
    prepare_turned(0)
    absorb1()
    y_step(1, 5)
    y_step(2, 2)
    y_step(3, 1)
    y_finish(1)
    prepare_ring(1)
    absorb4()
    y_step(2, 3)
    y_step(3, 2)
    z_finish(1)
    prepare_line(1)
    absorb2()
    y_step(2, 4)
    y_step(3, 3)
    y_step(2, 5)
    y_finish(2)
    prepare_ring(2)
    y_step(3, 4)
    y_step(3, 5)
    y_finish(3)
    new = lax.broadcasted_iota(I32, (128, 128), 0)
    old = reordered(new, (2, 3, 4, 0, 1, 5, 6))
    prepare_turned(3, one_hot(lax.broadcasted_iota(I32, (128, 128), 1), old))
    absorb3()
    absorb5(1 - core, True)
    absorb5(core, False)
    reduce()

    for copy in started:
        copy.wait_send()

    @pl.loop(1, 16)
    def _(k):
        for g in range(2):
            base_copy(g, k).wait_send()

    @pl.loop(0, 4)
    def _(q):
        t_copy(q).wait_send()

        @pl.loop(1, 16)
        def _(k):
            a_copy(q, k).wait_send()


def per_device(stem, left, right, slice_bits, leg_order):
    smem, vmem = pl.BlockSpec(memory_space=pltpu.SMEM), pl.BlockSpec(memory_space=pltpu.VMEM)
    shape = jax.ShapeDtypeStruct
    fz, fy, sel = pl.pallas_call(
        fragments,
        out_shape=(shape((2, 32, 512), F32), shape((4, 8, 2, 8, 256), F32), shape((4, 8, 256), I32)),
        in_specs=[smem, smem, vmem, vmem],
        out_specs=(vmem, vmem, vmem),
        compiler_params=pltpu.CompilerParams(vmem_limit_bytes=32 * 2**20),
    )(leg_order, slice_bits, left, right)
    dma = pltpu.SemaphoreType.DMA
    result = pl.pallas_call(
        contract,
        out_shape=shape((64, 256), F32),
        in_specs=[vmem, vmem, vmem, vmem],
        out_specs=vmem,
        scratch_shapes=[
            pltpu.VMEM((2, 16, 32, 512), F32),
            pltpu.VMEM((4, 8, 2, 16, 8, 256), F32),
            pltpu.VMEM((6, 512, 512), BF16),
            pltpu.VMEM((6, 512, 512), BF16),
            pltpu.VMEM((1024, 512), F32),
            pltpu.VMEM((2, 4, 2, 128, 256), F32),
            pltpu.VMEM((4, 4, 128, 256), F32),
            pltpu.VMEM((4, 16, 32, 256), F32),
            pltpu.VMEM((4, 16, 32, 256), F32),
            pltpu.VMEM((4, 4, 128, 256), F32),
            pltpu.VMEM((2, 4, 2, 8, 16, 256), F32),
            pltpu.VMEM((4, 2, 8, 16, 256), F32),
            pltpu.VMEM((2, 2, 4, 4, 16, 256), F32),
            pltpu.VMEM((2, 4, 16, 256), F32),
            pltpu.VMEM((4, 16, 256), F32),
            dma((2, 2, 2, 4)), dma((2, 2, 2, 4)), dma((2,)), dma((2,)),
            dma((2, 16)), dma((2, 16)), dma((4, 2, 4)), dma((4, 2, 4)), dma((4, 8)), dma((4, 8)),
            dma((4, 16)), dma((4, 16)), dma((4,)), dma((4,)), dma((2, 2, 4)), dma((2, 2, 4)), dma, dma,
        ],
        compiler_params=pltpu.CompilerParams(
            collective_id=0, has_side_effects=True, vmem_limit_bytes=56 * 2**20
        ),
    )(stem.reshape(1024, 512), fz, fy, sel)
    return result.reshape(16, 1, 1024)


def solution(mesh):
    in_specs = (
        P("cuts", "mode", None, None),
        P(None, None, "mode", None),
        P(),
        P("cuts", None),
        P(),
    )
    out_specs = P(None, "mode", "cuts")
    return jax.shard_map(per_device, mesh=mesh, in_specs=in_specs, out_specs=out_specs, check_vma=False)
```

```python
import functools

import jax
import jax.numpy as jnp
from jax import lax
from jax.experimental import pallas as pl
from jax.experimental.pallas import tpu as pltpu
from jax.sharding import PartitionSpec as P

F32, BF16, I32 = jnp.float32, jnp.bfloat16, jnp.int32
MESH = pl.DeviceIdType.MESH
LINE = (0, 2)
RING = (1, 3, 4, 5)
NATURAL9 = (0, 1, 2, 3, 4, 5, 6, 7, 8)
COLUMNS = {1: (8, 2, 3, 4, 5, 6, 7, 0, 1), 5: (7, 8, 0, 1, 2, 3, 4, 5, 6)}
ROWS = {1: (3, 4, 0, 1, 2), 5: (2, 1, 0, 3, 4)}


def halves(a):
    high = a.astype(BF16)
    return high, (a - high.astype(F32)).astype(BF16)


def dot(a, b, transposed=False):
    dims = (((1,), (1 if transposed else 0,)), ((), ()))
    return lax.dot_general(a, b, dims, preferred_element_type=F32)


def dot3(a, b, transposed=False):
    (ah, al), (bh, bl) = a, b
    return dot(ah, bl, transposed) + dot(al, bh, transposed) + dot(ah, bh, transposed)


def reordered(index, order):
    bits = len(order)
    total = jnp.zeros_like(index)
    for place, leg in enumerate(order):
        bit = jnp.right_shift(index, bits - 1 - place) & 1
        total = total + jnp.left_shift(bit, bits - 1 - leg)
    return total


def one_hot(rows, columns):
    return jnp.where(rows == columns, 1.0, 0.0).astype(BF16)


def contract(
    order, bits, stem_hbm, left_hbm, right_hbm, out,
    left, right, stem, product, fy, xh, xl_, gz, gy, bh, bl, y0, w, tt, rr, s3, acc, twin, part, final, last,
    in_sem, z_send, z_recv, x_send, x_recv, base_send, base_recv, y_send, y_recv, d_send, d_recv,
    a_send, a_recv, t_send, t_recv, r_send, r_recv, l_send, l_recv,
):
    c, m = lax.axis_index("cuts"), lax.axis_index("mode")
    xl, z = m // 8, lax.rem(m, 8)
    y, xh_, core = c // 4, lax.rem(c // 2, 2), lax.rem(c, 2)
    z_next = [(c, xl * 8 + lax.rem(z + 1, 8)), (c, xl * 8 + lax.rem(z + 7, 8))]
    y_next = [(lax.rem(y + 1, 8) * 4 + lax.rem(c, 4), m), (lax.rem(y + 7, 8) * 4 + lax.rem(c, 4), m)]
    sibling = (c + 1 - 2 * core, m)
    across = (c + 2 - 4 * xh_, m)
    beside = (c, m + 8 - 16 * xl)

    def peer(k):
        return lax.rem(m + k, 16)

    barrier = pltpu.get_barrier_semaphore()

    @pl.loop(1, 16)
    def _(k):
        pl.semaphore_signal(barrier, inc=1, device_id=(c, peer(k)), device_id_type=MESH)

    for target in (*y_next, sibling, across):
        pl.semaphore_signal(barrier, inc=1, device_id=target, device_id_type=MESH)

    loads = [
        pltpu.make_async_copy(src, dst, in_sem.at[n])
        for n, (src, dst) in enumerate(((right_hbm, right), (left_hbm, left), (stem_hbm, stem)))
    ]
    for load in loads:
        load.start()

    started = []

    def remote(src, dst, send, recv, target):
        return pltpu.make_async_remote_copy(
            src_ref=src, dst_ref=dst, send_sem=send, recv_sem=recv, device_id=target, device_id_type=MESH
        )

    def go(copy):
        copy.start()
        started.append(copy)

    def multiply():
        loads[0].wait()
        loads[1].wait()
        product[...] = dot3(halves(left[...].reshape(384, 512)), halves(right[...]))

    def fragment(t):
        value = product[64 * t : 64 * t + 64]
        first = value.astype(BF16)
        rest = value - first.astype(F32)
        second = rest.astype(BF16)
        third = (rest - second.astype(F32)).astype(BF16)
        stacked = jnp.concatenate([first, second, third], axis=0)
        spot = lax.broadcasted_iota(I32, (8, 512), 1)
        spot = reordered(spot, COLUMNS.get(t, NATURAL9))
        column = jnp.zeros_like(spot)
        for q in range(9):
            bit = jnp.right_shift(spot, jnp.full_like(spot, 8 - order[t, q])) & 1
            column = column + jnp.left_shift(bit, 8 - q)
        moved = dot(stacked, one_hot(lax.broadcasted_iota(I32, (512, 512), 0), column[0:1]))
        pieces = [moved[64 * k : 64 * k + 64] for k in range(3)]
        if t in ROWS:
            new = lax.broadcasted_iota(I32, (64, 64), 0)
            old = (new & 32) + reordered(new & 31, ROWS[t])
            turn = one_hot(lax.broadcasted_iota(I32, (64, 64), 1), old)
            pieces = [dot(turn, p.astype(BF16)) for p in pieces]
        value = pieces[0] + pieces[1] + pieces[2]
        if t in LINE:
            wide = jnp.full((32, 512), bits[0, t], I32)
            gz[LINE.index(t), m] = jnp.where(wide == 1, value[32:], value[:32])
        else:
            k = RING.index(t)
            for s in range(8):
                for h in range(2):
                    fy[k, s, h] = value[8 * s : 8 * s + 8, 256 * h : 256 * h + 256]
            gy[k, y, core, m] = fy[k, y, core]

    def split_stem():
        loads[2].wait()
        upper = lax.broadcasted_iota(I32, (8, 512), 0) < 4

        @pl.loop(0, 16)
        def _(i):
            for m4 in range(2):
                a = [stem[8 * m4 : 8 * m4 + 8, pl.ds(pl.multiple_of(2048 * i, 2048) + 512 * j, 512)] for j in range(4)]
                low = [jnp.where(upper, a[j], pltpu.roll(a[j + 1], 4, 0)) for j in (0, 2)]
                high = [jnp.where(upper, pltpu.roll(a[j], 4, 0), a[j + 1]) for j in (0, 2)]
                for m5, tiles in enumerate((low, high)):
                    rows = pl.ds(pl.multiple_of(256 * (2 * m4 + m5) + 16 * i, 16), 16)
                    xh[rows], xl_[rows] = halves(jnp.concatenate(tiles, axis=0))

    def x_copy(k, n):
        if n == 0:
            owner = z
        elif n == 7:
            owner = lax.rem(z + 4, 8)
        else:
            owner = lax.rem(z + 8 - (1 - 2 * ((n - 1) % 2)) * ((n + 1) // 2), 8)
        piece = gz.at[k, xl * 8 + owner]
        return remote(piece, piece, x_send.at[k, n], x_recv.at[k, n], beside)

    def z_copy(k, cls, d, s):
        owner = lax.rem(z + 8 - (1 - 2 * d) * (s - 1), 8)
        row = (xl * 8 if cls == 0 else (1 - xl) * 8) + owner
        piece = gz.at[k, row]
        if s == 4:
            piece = gz.at[k, row, pl.ds(16 * d, 16)]
        return remote(piece, piece, z_send.at[k, cls, d, s - 1], z_recv.at[k, cls, d, s - 1], z_next[d])

    def z_first(k):
        go(x_copy(k, 0))
        for d in range(2):
            go(z_copy(k, 0, d, 1))

    def z_other(k):
        x_copy(k, 0).wait_recv()
        for d in range(2):
            go(z_copy(k, 1, d, 1))

    def z_step(k, s):
        for cls in range(2 if k == 0 else 1):
            for d in range(2):
                z_copy(k, cls, d, s - 1).wait_recv()
                if s < 5:
                    go(z_copy(k, cls, d, s))
                    if k == 1:
                        go(x_copy(k, 2 * (s - 1) - 1 + d))
        if k == 1 and s == 5:
            go(x_copy(k, 7))

    def z_finish(k):
        if k == 0:
            z_step(0, 5)
        else:
            for n in range(8):
                x_copy(k, n).wait_recv()

    def base_copy(g, k):
        pair = pl.ds(2 * g, 2)
        return remote(
            fy.at[pair, y, core], gy.at[pair, y, core, m],
            base_send.at[g, k], base_recv.at[g, k], (c, peer(k)),
        )

    def base_start(g):
        @pl.loop(1, 16)
        def _(k):
            base_copy(g, k).start()

    def base_wait(g):
        @pl.loop(1, 16)
        def _(k):
            base_copy(g, k).wait_recv()

    def y_copy(t, d, s):
        owner = lax.rem(y + 8 - (1 - 2 * d) * (s - 1), 8)
        piece = gy.at[t, owner, core]
        if s == 4:
            piece = gy.at[t, owner, core, pl.ds(8 * d, 8)]
        return remote(piece, piece, y_send.at[t, d, s - 1], y_recv.at[t, d, s - 1], y_next[d])

    def d_copy(t, n):
        if n == 0:
            slot = y
        elif n == 7:
            slot = lax.rem(y + 4, 8)
        else:
            slot = lax.rem(y + 8 - (1 - 2 * ((n - 1) % 2)) * ((n + 1) // 2), 8)
        piece = gy.at[t, slot, core]
        return remote(piece, piece, d_send.at[t, n], d_recv.at[t, n], sibling)

    def y_step(t, s):
        if s == 1:
            if t % 2 == 0:
                base_wait(t // 2)
            for d in range(2):
                go(y_copy(t, d, 1))
            go(d_copy(t, 0))
            return
        for d in range(2):
            y_copy(t, d, s - 1).wait_recv()
            if s < 5:
                go(y_copy(t, d, s))
                go(d_copy(t, 2 * (s - 1) - 1 + d))
        if s == 5:
            go(d_copy(t, 7))

    def y_finish(t):
        for n in range(8):
            d_copy(t, n).wait_recv()

    def prepare_line(k):
        b = LINE[k]

        @pl.loop(0, 4)
        def _(i):
            rows = pl.ds(pl.multiple_of(128 * i, 128), 128)
            bh[b, rows], bl[b, rows] = halves(gz[k, pl.ds(4 * i, 4)].reshape(128, 512))

    def prepare_ring(t):
        b = RING[t]
        one = jnp.full((8, 256), bits[0, b], I32) == 1

        @pl.loop(0, 16)
        def _(i):
            rows = pl.ds(pl.multiple_of(32 * i, 32), 32)
            for h in range(2):
                lanes = slice(256 * h, 256 * h + 256)
                value = jnp.concatenate(
                    [jnp.where(one, gy[t, 4 + q, h, i], gy[t, q, h, i]) for q in range(4)], axis=0
                )
                bh[b, rows, lanes], bl[b, rows, lanes] = halves(value)

    def prepare_turned(t, turn=None):
        b = RING[t]
        one = jnp.full((1, 8, 256), bits[0, b], I32) == 1

        @pl.loop(0, 4)
        def _(q):
            rows = pl.ds(pl.multiple_of(128 * q, 128), 128)
            for h in range(2):
                lanes = slice(256 * h, 256 * h + 256)
                value = jnp.where(one, gy[t, 4 + q, h], gy[t, q, h]).reshape(128, 256)
                high, low = halves(value)
                if turn is not None:
                    high, low = dot(turn, high).astype(BF16), dot(turn, low).astype(BF16)
                bh[b, rows, lanes], bl[b, rows, lanes] = high, low

    def matrix(b):
        return bh[b], bl[b]

    def absorb0():
        @pl.loop(0, 2)
        def _(i):
            rows = pl.ds(pl.multiple_of(512 * i, 512), 512)
            y0[rows] = dot3((xh[rows], xl_[rows]), matrix(0), True)

    def absorb1():
        @pl.loop(0, 4)
        def _(i):
            rows = pl.ds(pl.multiple_of(256 * i, 256), 256)
            data = jnp.concatenate([y0[rows, :256], y0[rows, 256:]], axis=0)
            w[:, i] = dot3(matrix(1), halves(data)).reshape(4, 128, 256)

    def a_copy(q, k):
        return remote(
            tt.at[q, peer(k)], rr.at[q, m], a_send.at[q, k], a_recv.at[q, k], (c, peer(k))
        )

    def absorb2():
        @pl.loop(0, 4)
        def _(q):
            new = dot3(matrix(2), halves(w[q].reshape(512, 256)))
            tt[q] = new.reshape(16, 32, 256)
            rr[q, m] = tt[q, m]

            @pl.loop(1, 16)
            def _(k):
                a_copy(q, k).start()

    def absorb34():
        @pl.loop(0, 2)
        def _(m13):
            @pl.loop(0, 2)
            def _(h):
                q = 2 * m13 + h

                @pl.loop(1, 16)
                def _(k):
                    a_copy(q, k).wait_recv()

                s3[h] = dot3(matrix(3), halves(rr[q].reshape(512, 256)))

            data = jnp.concatenate([s3[0], s3[1]], axis=1)
            new = dot3(halves(data), matrix(4), True)
            for h in range(2):
                w[2 * m13 + h] = new[:, 256 * h : 256 * h + 256].reshape(4, 128, 256)

    def t_copy(i):
        return remote(acc.at[1 - core, i], twin.at[i], t_send.at[i], t_recv.at[i], sibling)

    def absorb5(half, send):
        rows = pl.ds(pl.multiple_of(256 * half, 256), 256)

        @pl.loop(0, 4)
        def _(i):
            data = w[:, i].reshape(512, 256)
            new = dot3((bh[5, rows], bl[5, rows]), halves(data)).reshape(2, 8, 16, 256)
            if send:
                acc[half, i] = new
                t_copy(i).start()
            else:
                t_copy(i).wait_recv()
                acc[half, i] = new + twin[i]

    def steps(k, d):
        return 4 if k == d else 3

    def r_copy(k, d, s):
        n = steps(k, d)
        dest = lax.rem(y + 8 + (1 - 2 * d) * (n - s + 1), 8)
        src = acc.at[core, :, k, dest] if s == 1 else part.at[k, d, s - 2]
        return remote(src, part.at[k, d, s - 1], r_send.at[k, d, s - 1], r_recv.at[k, d, s - 1], y_next[d])

    def reduce():
        order = [(k, d) for d in range(2) for k in range(2)]
        for k, d in order:
            go(r_copy(k, d, 1))
        for s in range(2, 5):
            for k, d in order:
                n = steps(k, d)
                if s <= n:
                    dest = lax.rem(y + 8 + (1 - 2 * d) * (n - s + 1), 8)
                    r_copy(k, d, s - 1).wait_recv()
                    part[k, d, s - 2] = part[k, d, s - 2] + acc[core, :, k, dest]
                    go(r_copy(k, d, s))
        for k in range(2):
            for d in range(2):
                r_copy(k, d, steps(k, d)).wait_recv()
            final[k] = acc[core, :, k, y] + part[k, 0, steps(k, 0) - 1] + part[k, 1, steps(k, 1) - 1]
        swap = remote(final.at[1 - xh_], last, l_send, l_recv, across)
        go(swap)
        swap.wait_recv()
        for i in range(4):
            value = final[xh_, i] + last[i]
            for n in range(4):
                out[4 * i : 4 * i + 4, 256 * n : 256 * n + 256] = value[4 * n : 4 * n + 4]

    multiply()
    fragment(0)
    fragment(1)
    fragment(3)
    pl.semaphore_wait(barrier, 19)
    z_first(0)
    base_start(0)
    fragment(2)
    z_other(0)
    y_step(0, 1)
    fragment(4)
    fragment(5)
    z_step(0, 2)
    z_first(1)
    y_step(0, 2)
    split_stem()
    z_step(0, 3)
    y_step(0, 3)
    z_step(1, 2)
    base_start(1)
    z_step(0, 4)
    y_step(0, 4)
    z_step(1, 3)
    y_step(1, 1)
    y_step(0, 5)
    z_finish(0)
    z_step(1, 4)
    y_step(2, 1)
    prepare_line(0)
    absorb0()
    y_step(1, 2)
    z_step(1, 5)
    y_step(2, 2)
    y_finish(0)
    prepare_turned(0)
    absorb1()
    y_step(1, 3)
    y_step(2, 3)
    z_finish(1)
    prepare_line(1)
    absorb2()
    y_step(1, 4)
    y_step(2, 4)
    y_step(3, 1)
    y_step(1, 5)
    y_step(2, 5)
    y_step(3, 2)
    y_finish(1)
    prepare_ring(1)
    y_step(3, 3)
    y_finish(2)
    prepare_ring(2)
    y_step(3, 4)
    y_step(3, 5)
    y_finish(3)
    new = lax.broadcasted_iota(I32, (128, 128), 0)
    old = reordered(new, (2, 3, 4, 5, 6, 0, 1))
    prepare_turned(3, one_hot(lax.broadcasted_iota(I32, (128, 128), 1), old))
    absorb34()
    absorb5(1 - core, True)
    absorb5(core, False)
    reduce()

    for copy in started:
        copy.wait_send()

    @pl.loop(1, 16)
    def _(k):
        for g in range(2):
            base_copy(g, k).wait_send()

    @pl.loop(0, 4)
    def _(q):
        t_copy(q).wait_send()

        @pl.loop(1, 16)
        def _(k):
            a_copy(q, k).wait_send()


def per_device(stem, left, right, slice_bits, leg_order):
    smem, anywhere = pl.BlockSpec(memory_space=pltpu.SMEM), pl.BlockSpec(memory_space=pl.ANY)
    dma = pltpu.SemaphoreType.DMA
    result = pl.pallas_call(
        contract,
        out_shape=jax.ShapeDtypeStruct((16, 1024), F32),
        in_specs=[smem, smem, anywhere, anywhere, anywhere],
        out_specs=pl.BlockSpec(memory_space=pltpu.VMEM),
        scratch_shapes=[
            pltpu.VMEM((6, 2, 32, 512), F32),
            pltpu.VMEM((512, 512), F32),
            pltpu.VMEM((16, 32768), F32),
            pltpu.VMEM((384, 512), F32),
            pltpu.VMEM((4, 8, 2, 8, 256), F32),
            pltpu.VMEM((1024, 512), BF16),
            pltpu.VMEM((1024, 512), BF16),
            pltpu.VMEM((2, 16, 32, 512), F32),
            pltpu.VMEM((4, 8, 2, 16, 8, 256), F32),
            pltpu.VMEM((6, 512, 512), BF16),
            pltpu.VMEM((6, 512, 512), BF16),
            pltpu.VMEM((1024, 512), F32),
            pltpu.VMEM((4, 4, 128, 256), F32),
            pltpu.VMEM((4, 16, 32, 256), F32),
            pltpu.VMEM((4, 16, 32, 256), F32),
            pltpu.VMEM((2, 512, 256), F32),
            pltpu.VMEM((2, 4, 2, 8, 16, 256), F32),
            pltpu.VMEM((4, 2, 8, 16, 256), F32),
            pltpu.VMEM((2, 2, 4, 4, 16, 256), F32),
            pltpu.VMEM((2, 4, 16, 256), F32),
            pltpu.VMEM((4, 16, 256), F32),
            dma((3,)), dma((2, 2, 2, 4)), dma((2, 2, 2, 4)), dma((2, 8)), dma((2, 8)),
            dma((2, 16)), dma((2, 16)), dma((4, 2, 4)), dma((4, 2, 4)), dma((4, 8)), dma((4, 8)),
            dma((4, 16)), dma((4, 16)), dma((4,)), dma((4,)), dma((2, 2, 4)), dma((2, 2, 4)), dma, dma,
        ],
        compiler_params=pltpu.CompilerParams(
            collective_id=0, has_side_effects=True, vmem_limit_bytes=56 * 2**20
        ),
    )(leg_order, slice_bits, stem.reshape(16, 32768), left, right)
    return result.reshape(16, 1, 1024)


def solution(mesh):
    in_specs = (
        P("cuts", "mode", None, None),
        P(None, None, "mode", None),
        P(),
        P("cuts", None),
        P(),
    )
    out_specs = P(None, "mode", "cuts")
    return jax.shard_map(per_device, mesh=mesh, in_specs=in_specs, out_specs=out_specs, check_vma=False)
```

```python
import functools

import jax
import jax.numpy as jnp
from jax import lax
from jax.experimental import pallas as pl
from jax.experimental.pallas import tpu as pltpu
from jax.sharding import PartitionSpec as P

F32, BF16, I32 = jnp.float32, jnp.bfloat16, jnp.int32
MESH = pl.DeviceIdType.MESH
LINE = (0,)
RING = (1, 2, 3, 4, 5)
GROUPS = ((0, 1), (1, 2), (3, 2))
NATURAL9 = (0, 1, 2, 3, 4, 5, 6, 7, 8)
COLUMNS = {1: (8, 2, 3, 4, 5, 6, 7, 0, 1), 5: (7, 8, 0, 1, 2, 3, 4, 5, 6)}
ROWS = {1: (3, 4, 0, 1, 2), 5: (2, 1, 0, 3, 4)}


def halves(a):
    high = a.astype(BF16)
    return high, (a - high.astype(F32)).astype(BF16)


def dot(a, b, transposed=False):
    dims = (((1,), (1 if transposed else 0,)), ((), ()))
    return lax.dot_general(a, b, dims, preferred_element_type=F32)


def dot3(a, b, transposed=False):
    (ah, al), (bh, bl) = a, b
    return dot(ah, bl, transposed) + dot(al, bh, transposed) + dot(ah, bh, transposed)


def reordered(index, order):
    bits = len(order)
    total = jnp.zeros_like(index)
    for place, leg in enumerate(order):
        bit = jnp.right_shift(index, bits - 1 - place) & 1
        total = total + jnp.left_shift(bit, bits - 1 - leg)
    return total


def one_hot(rows, columns):
    return jnp.where(rows == columns, 1.0, 0.0).astype(BF16)


def contract(
    order, bits, stem_hbm, left_hbm, right_hbm, out,
    left, right, stem, product, fy, xh, xl_, gz, gy, bh, bl, y0, w, tt, rr, s3, acc, twin, part, final, last,
    in_sem, z_send, z_recv, x_send, x_recv, base_send, base_recv, y_send, y_recv, d_send, d_recv,
    e_send, e_recv, f_send,
    a_send, a_recv, t_send, t_recv, r_send, r_recv, l_send, l_recv,
):
    c, m = lax.axis_index("cuts"), lax.axis_index("mode")
    xl, z = m // 8, lax.rem(m, 8)
    y, xh_, core = c // 4, lax.rem(c // 2, 2), lax.rem(c, 2)
    z_next = [(c, xl * 8 + lax.rem(z + 1, 8)), (c, xl * 8 + lax.rem(z + 7, 8))]
    y_next = [(lax.rem(y + 1, 8) * 4 + lax.rem(c, 4), m), (lax.rem(y + 7, 8) * 4 + lax.rem(c, 4), m)]
    sibling = (c + 1 - 2 * core, m)
    across = (c + 2 - 4 * xh_, m)
    beside = (c, m + 8 - 16 * xl)
    corner = (c + 2 - 4 * xh_, m + 8 - 16 * xl)

    def peer(k):
        return lax.rem(m + k, 16)

    barrier = pltpu.get_barrier_semaphore()

    @pl.loop(1, 16)
    def _(k):
        pl.semaphore_signal(barrier, inc=1, device_id=(c, peer(k)), device_id_type=MESH)

    for target in (*y_next, sibling, across, corner):
        pl.semaphore_signal(barrier, inc=1, device_id=target, device_id_type=MESH)

    loads = [
        pltpu.make_async_copy(src, dst, in_sem.at[n])
        for n, (src, dst) in enumerate(((right_hbm, right), (left_hbm, left), (stem_hbm, stem)))
    ]
    for load in loads:
        load.start()

    def remote(src, dst, send, recv, target):
        return pltpu.make_async_remote_copy(
            src_ref=src, dst_ref=dst, send_sem=send, recv_sem=recv, device_id=target, device_id_type=MESH
        )

    def settle(ref, sem):
        pltpu.make_async_copy(ref, ref, sem).wait()

    def go(copy):
        copy.start()

    def multiply():
        loads[0].wait()
        loads[1].wait()
        product[...] = dot3(halves(left[...].reshape(384, 512)), halves(right[...]))

    def fragment(t):
        value = product[64 * t : 64 * t + 64]
        first = value.astype(BF16)
        rest = value - first.astype(F32)
        second = rest.astype(BF16)
        third = (rest - second.astype(F32)).astype(BF16)
        stacked = jnp.concatenate([first, second, third], axis=0)
        spot = lax.broadcasted_iota(I32, (8, 512), 1)
        spot = reordered(spot, COLUMNS.get(t, NATURAL9))
        column = jnp.zeros_like(spot)
        for q in range(9):
            bit = jnp.right_shift(spot, jnp.full_like(spot, 8 - order[t, q])) & 1
            column = column + jnp.left_shift(bit, 8 - q)
        moved = dot(stacked, one_hot(lax.broadcasted_iota(I32, (512, 512), 0), column[0:1]))
        pieces = [moved[64 * k : 64 * k + 64] for k in range(3)]
        if t in ROWS:
            new = lax.broadcasted_iota(I32, (64, 64), 0)
            old = (new & 32) + reordered(new & 31, ROWS[t])
            turn = one_hot(lax.broadcasted_iota(I32, (64, 64), 1), old)
            pieces = [dot(turn, p.astype(BF16)) for p in pieces]
        value = pieces[0] + pieces[1] + pieces[2]
        if t in LINE:
            wide = jnp.full((32, 512), bits[0, t], I32)
            gz[m] = jnp.where(wide == 1, value[32:], value[:32])
        else:
            k = RING.index(t)
            for s in range(8):
                for h in range(2):
                    fy[k, s, h] = value[8 * s : 8 * s + 8, 256 * h : 256 * h + 256]
            gy[k, y, core, m] = fy[k, y, core]

    def split_stem():
        loads[2].wait()
        upper = lax.broadcasted_iota(I32, (8, 512), 0) < 4

        @pl.loop(0, 16)
        def _(i):
            for m4 in range(2):
                a = [stem[8 * m4 : 8 * m4 + 8, pl.ds(pl.multiple_of(2048 * i, 2048) + 512 * j, 512)] for j in range(4)]
                low = [jnp.where(upper, a[j], pltpu.roll(a[j + 1], 4, 0)) for j in (0, 2)]
                high = [jnp.where(upper, pltpu.roll(a[j], 4, 0), a[j + 1]) for j in (0, 2)]
                for m5, tiles in enumerate((low, high)):
                    rows = pl.ds(pl.multiple_of(256 * (2 * m4 + m5) + 16 * i, 16), 16)
                    xh[rows], xl_[rows] = halves(jnp.concatenate(tiles, axis=0))

    def x_copy():
        return remote(gz.at[m], gz.at[m], x_send, x_recv, beside)

    def z_copy(cls, d, s):
        owner = lax.rem(z + 8 - (1 - 2 * d) * (s - 1), 8)
        row = (xl * 8 if cls == 0 else (1 - xl) * 8) + owner
        piece = gz.at[row]
        if s == 4:
            piece = gz.at[row, pl.ds(16 * d, 16)]
        return remote(piece, piece, z_send, z_recv.at[cls, d, s - 1], z_next[d])

    def z_first():
        go(x_copy())
        for d in range(2):
            go(z_copy(0, d, 1))

    def z_other():
        x_copy().wait_recv()
        for d in range(2):
            go(z_copy(1, d, 1))

    def z_step(s):
        for cls in range(2):
            for d in range(2):
                z_copy(cls, d, s - 1).wait_recv()
                if s < 5:
                    go(z_copy(cls, d, s))

    def base_copy(g, k):
        pair = pl.ds(*GROUPS[g])
        return remote(
            fy.at[pair, y, core], gy.at[pair, y, core, m],
            base_send, base_recv.at[g], (c, xl * 8 + lax.rem(z + k, 8)),
        )

    def base_start(g):
        @pl.loop(1, 8)
        def _(k):
            base_copy(g, k).start()

    def base_wait(g):
        settle(gy.at[pl.ds(*GROUPS[g]), y, core, pl.ds(0, 7)], base_recv.at[g])

    def y_copy(t, d, s):
        owner = lax.rem(y + 8 - (1 - 2 * d) * (s - 1), 8)
        piece = gy.at[t, owner, core, pl.ds(8 * xl, 8)]
        if s == 4:
            piece = gy.at[t, owner, core, pl.ds(8 * xl + 4 * d, 4)]
        return remote(piece, piece, y_send, y_recv.at[t, d, s - 1], y_next[d])

    def slot(n):
        if n == 0:
            return y
        if n == 7:
            return lax.rem(y + 4, 8)
        return lax.rem(y + 8 - (1 - 2 * ((n - 1) % 2)) * ((n + 1) // 2), 8)

    def d_copy(t, n):
        piece = gy.at[t, slot(n), core, pl.ds(8 * xl, 8)]
        return remote(piece, piece, d_send, d_recv.at[t], sibling)

    def e_copy(t, n, e):
        piece = gy.at[t, slot(n), core, pl.ds(8 * xl + 4 * e, 4)]
        return remote(piece, piece, e_send, e_recv.at[t, n], corner if e else beside)

    def f_copy(t, n):
        piece = gy.at[t, slot(n), core, pl.ds(8 - 8 * xl, 8)]
        return remote(piece, piece, f_send, d_recv.at[t], sibling)

    def share(t, n):
        for e in range(2):
            go(e_copy(t, n, e))
        go(d_copy(t, n))

    def relay(t, n):
        settle(gy.at[t, slot(n), core, pl.ds(8 - 8 * xl, 8)], e_recv.at[t, n])
        go(f_copy(t, n))

    def y_step(t, s):
        if s == 1:
            for g, (first, _) in enumerate(GROUPS):
                if t == first:
                    base_wait(g)
            for d in range(2):
                go(y_copy(t, d, 1))
            share(t, 0)
            return
        for d in range(2):
            y_copy(t, d, s - 1).wait_recv()
            if s < 5:
                go(y_copy(t, d, s))
        if s < 5:
            for d in range(2):
                share(t, 2 * s - 3 + d)
        else:
            share(t, 7)
        for n in (0,) if s == 2 else (2 * s - 5, 2 * s - 4):
            relay(t, n)

    def y_finish(t):
        settle(gy.at[t, :, 1 - core], d_recv.at[t])

    def prepare_line(k):
        b = LINE[k]

        @pl.loop(0, 4)
        def _(i):
            rows = pl.ds(pl.multiple_of(128 * i, 128), 128)
            bh[b, rows], bl[b, rows] = halves(gz[pl.ds(4 * i, 4)].reshape(128, 512))

    def prepare_ring(t):
        b = RING[t]
        one = jnp.full((8, 256), bits[0, b], I32) == 1

        @pl.loop(0, 16)
        def _(i):
            rows = pl.ds(pl.multiple_of(32 * i, 32), 32)
            for h in range(2):
                lanes = slice(256 * h, 256 * h + 256)
                value = jnp.concatenate(
                    [jnp.where(one, gy[t, 4 + q, h, i], gy[t, q, h, i]) for q in range(4)], axis=0
                )
                bh[b, rows, lanes], bl[b, rows, lanes] = halves(value)

    def prepare_turned(t, turn=None):
        b = RING[t]
        one = jnp.full((1, 8, 256), bits[0, b], I32) == 1

        @pl.loop(0, 4)
        def _(q):
            rows = pl.ds(pl.multiple_of(128 * q, 128), 128)
            for h in range(2):
                lanes = slice(256 * h, 256 * h + 256)
                value = jnp.where(one, gy[t, 4 + q, h], gy[t, q, h]).reshape(128, 256)
                high, low = halves(value)
                if turn is not None:
                    high, low = dot(turn, high).astype(BF16), dot(turn, low).astype(BF16)
                bh[b, rows, lanes], bl[b, rows, lanes] = high, low

    def matrix(b):
        return bh[b], bl[b]

    def absorb0():
        @pl.loop(0, 2)
        def _(i):
            rows = pl.ds(pl.multiple_of(512 * i, 512), 512)
            y0[rows] = dot3((xh[rows], xl_[rows]), matrix(0), True)

    def absorb1():
        @pl.loop(0, 4)
        def _(i):
            rows = pl.ds(pl.multiple_of(256 * i, 256), 256)
            data = jnp.concatenate([y0[rows, :256], y0[rows, 256:]], axis=0)
            w[:, i] = dot3(matrix(1), halves(data)).reshape(4, 128, 256)

    def a_copy(q, k):
        return remote(
            tt.at[q, peer(k)], rr.at[q, m], a_send, a_recv.at[q], (c, peer(k))
        )

    def absorb2():
        @pl.loop(0, 4)
        def _(q):
            new = dot3(matrix(2), halves(w[q].reshape(512, 256)))
            tt[q] = new.reshape(16, 32, 256)
            rr[q, m] = tt[q, m]

            @pl.loop(1, 16)
            def _(k):
                a_copy(q, k).start()

    def absorb34():
        @pl.loop(0, 2)
        def _(m13):
            @pl.loop(0, 2)
            def _(h):
                q = 2 * m13 + h

                settle(rr.at[q, pl.ds(0, 15)], a_recv.at[q])
                s3[h] = dot3(matrix(3), halves(rr[q].reshape(512, 256)))

            data = jnp.concatenate([s3[0], s3[1]], axis=1)
            new = dot3(halves(data), matrix(4), True)
            for h in range(2):
                w[2 * m13 + h] = new[:, 256 * h : 256 * h + 256].reshape(4, 128, 256)

    def t_copy(i):
        return remote(acc.at[1 - core, i], twin.at[i], t_send, t_recv.at[i], sibling)

    def absorb5(half, low, send):
        rows = pl.ds(pl.multiple_of(256 * half, 256), 256)

        @pl.loop(low, low + 2)
        def _(i):
            data = w[:, i].reshape(512, 256)
            new = dot3((bh[5, rows], bl[5, rows]), halves(data)).reshape(2, 8, 16, 256)
            if send:
                acc[half, i] = new
                t_copy(i).start()
            else:
                t_copy(i).wait_recv()
                acc[half, i] = new + twin[i]

    CHAINS = ((0, 0), (1, 1), (0, 1), (1, 0))

    def steps(k, d):
        return 4 if k == d else 3

    def r_dest(k, d, s):
        return lax.rem(y + 8 + (1 - 2 * d) * (steps(k, d) - s + 1), 8)

    def r_copy(p, k, d, s):
        src = acc.at[core, pl.ds(2 * p, 2), k, r_dest(k, d, s)] if s == 1 else part.at[p, k, d, s - 2]
        return remote(
            src, part.at[p, k, d, s - 1], r_send, r_recv.at[p, k, d, s - 1], y_next[d]
        )

    def r_step(p, s):
        for k, d in CHAINS:
            if s <= steps(k, d):
                if s > 1:
                    r_copy(p, k, d, s - 1).wait_recv()
                    part[p, k, d, s - 2] += acc[core, 2 * p : 2 * p + 2, k, r_dest(k, d, s)]
                go(r_copy(p, k, d, s))

    def l_copy(p):
        return remote(final.at[p, 1 - xh_], last.at[p], l_send, l_recv.at[p], across)

    def r_finish(p):
        for k in range(2):
            for d in range(2):
                r_copy(p, k, d, steps(k, d)).wait_recv()
            total = part[p, k, 0, steps(k, 0) - 1] + part[p, k, 1, steps(k, 1) - 1]
            final[p, k] = acc[core, 2 * p : 2 * p + 2, k, y] + total
        go(l_copy(p))

    def write(p):
        l_copy(p).wait_recv()
        for i in range(2):
            value = final[p, xh_, i] + last[p, i]
            rows = slice(8 * p + 4 * i, 8 * p + 4 * i + 4)
            for n in range(4):
                out[rows, 256 * n : 256 * n + 256] = value[4 * n : 4 * n + 4]

    multiply()
    fragment(0)
    fragment(1)
    pl.semaphore_wait(barrier, 20)
    z_first()
    base_start(0)
    fragment(2)
    fragment(3)
    base_start(1)
    fragment(4)
    fragment(5)
    z_other()
    y_step(0, 1)
    z_step(2)
    y_step(0, 2)
    y_step(1, 1)
    z_step(3)
    y_step(0, 3)
    y_step(1, 2)
    split_stem()
    y_step(0, 4)
    z_step(4)
    base_start(2)
    y_step(1, 3)
    y_step(0, 5)
    z_step(5)
    y_step(1, 4)
    relay(0, 7)
    prepare_line(0)
    absorb0()
    y_step(1, 5)
    y_finish(0)
    prepare_turned(0)
    relay(1, 7)
    absorb1()
    y_finish(1)
    prepare_ring(1)
    absorb2()
    y_step(2, 1)
    y_step(3, 1)
    y_step(2, 2)
    y_step(3, 2)
    y_step(4, 1)
    y_step(2, 3)
    y_step(3, 3)
    y_step(4, 2)
    y_step(2, 4)
    y_step(3, 4)
    y_step(4, 3)
    y_step(2, 5)
    y_step(3, 5)
    relay(2, 7)
    relay(3, 7)
    y_step(4, 4)
    y_finish(2)
    prepare_ring(2)
    y_step(4, 5)
    y_finish(3)
    prepare_ring(3)
    relay(4, 7)
    y_finish(4)
    new = lax.broadcasted_iota(I32, (128, 128), 0)
    old = reordered(new, (2, 3, 4, 5, 6, 0, 1))
    prepare_turned(4, one_hot(lax.broadcasted_iota(I32, (128, 128), 1), old))
    absorb34()
    for p in range(2):
        absorb5(1 - core, 2 * p, True)
        absorb5(core, 2 * p, False)
        r_step(p, 1)
    for s in range(2, 5):
        for p in range(2):
            r_step(p, s)
    for p in range(2):
        r_finish(p)
    for p in range(2):
        write(p)

    x_copy().wait_send()
    settle(gz.at[pl.ds(0, 14)], z_send)
    settle(fy.at[:, pl.ds(0, 7), 0], base_send)
    settle(gy.at[:, pl.ds(0, 7), 0, pl.ds(0, 8)], y_send)
    for sem in (d_send, e_send, f_send):
        settle(gy.at[:, :, 0, pl.ds(0, 8)], sem)
    settle(tt.at[:, pl.ds(0, 15)], a_send)
    settle(acc.at[0], t_send)
    settle(tt.at[:, pl.ds(0, 7)], r_send)
    settle(last, l_send)


def per_device(stem, left, right, slice_bits, leg_order):
    smem, anywhere = pl.BlockSpec(memory_space=pltpu.SMEM), pl.BlockSpec(memory_space=pl.ANY)
    dma = pltpu.SemaphoreType.DMA
    result = pl.pallas_call(
        contract,
        out_shape=jax.ShapeDtypeStruct((16, 1024), F32),
        in_specs=[smem, smem, anywhere, anywhere, anywhere],
        out_specs=pl.BlockSpec(memory_space=pltpu.VMEM),
        scratch_shapes=[
            pltpu.VMEM((6, 2, 32, 512), F32),
            pltpu.VMEM((512, 512), F32),
            pltpu.VMEM((16, 32768), F32),
            pltpu.VMEM((384, 512), F32),
            pltpu.VMEM((5, 8, 2, 8, 256), F32),
            pltpu.VMEM((1024, 512), BF16),
            pltpu.VMEM((1024, 512), BF16),
            pltpu.VMEM((16, 32, 512), F32),
            pltpu.VMEM((5, 8, 2, 16, 8, 256), F32),
            pltpu.VMEM((6, 512, 512), BF16),
            pltpu.VMEM((6, 512, 512), BF16),
            pltpu.VMEM((1024, 512), F32),
            pltpu.VMEM((4, 4, 128, 256), F32),
            pltpu.VMEM((4, 16, 32, 256), F32),
            pltpu.VMEM((4, 16, 32, 256), F32),
            pltpu.VMEM((2, 512, 256), F32),
            pltpu.VMEM((2, 4, 2, 8, 16, 256), F32),
            pltpu.VMEM((4, 2, 8, 16, 256), F32),
            pltpu.VMEM((2, 2, 2, 4, 2, 16, 256), F32),
            pltpu.VMEM((2, 2, 2, 16, 256), F32),
            pltpu.VMEM((2, 2, 16, 256), F32),
            dma((3,)), dma, dma((2, 2, 4)), dma, dma,
            dma, dma((3,)), dma, dma((5, 2, 4)), dma, dma((5,)),
            dma, dma((5, 8)), dma,
            dma, dma((4,)), dma, dma((4,)),
            dma, dma((2, 2, 2, 4)), dma, dma((2,)),
        ],
        compiler_params=pltpu.CompilerParams(
            collective_id=0, has_side_effects=True, vmem_limit_bytes=56 * 2**20
        ),
    )(leg_order, slice_bits, stem.reshape(16, 32768), left, right)
    return result.reshape(16, 1, 1024)


def solution(mesh):
    in_specs = (
        P("cuts", "mode", None, None),
        P(None, None, "mode", None),
        P(),
        P("cuts", None),
        P(),
    )
    out_specs = P(None, "mode", "cuts")
    return jax.shard_map(per_device, mesh=mesh, in_specs=in_specs, out_specs=out_specs, check_vma=False)
```

```python
import functools

import jax
import jax.numpy as jnp
from jax import lax
from jax.experimental import pallas as pl
from jax.experimental.pallas import tpu as pltpu
from jax.sharding import PartitionSpec as P

F32, BF16, I32 = jnp.float32, jnp.bfloat16, jnp.int32
MESH = pl.DeviceIdType.MESH
LINE = (0,)
RING = (1, 2, 3, 4, 5)
GROUPS = ((0, 1), (1, 2), (3, 2))
NATURAL9 = (0, 1, 2, 3, 4, 5, 6, 7, 8)
COLUMNS = {1: (8, 2, 3, 4, 5, 6, 7, 0, 1), 5: (7, 8, 0, 1, 2, 3, 4, 5, 6)}
ROWS = {1: (3, 4, 0, 1, 2), 5: (2, 1, 0, 3, 4)}


def halves(a):
    high = a.astype(BF16)
    return high, (a - high.astype(F32)).astype(BF16)


def dot(a, b, transposed=False):
    dims = (((1,), (1 if transposed else 0,)), ((), ()))
    return lax.dot_general(a, b, dims, preferred_element_type=F32)


def dot3(a, b, transposed=False):
    (ah, al), (bh, bl) = a, b
    return dot(ah, bl, transposed) + dot(al, bh, transposed) + dot(ah, bh, transposed)


def reordered(index, order):
    bits = len(order)
    total = jnp.zeros_like(index)
    for place, leg in enumerate(order):
        bit = jnp.right_shift(index, bits - 1 - place) & 1
        total = total + jnp.left_shift(bit, bits - 1 - leg)
    return total


def one_hot(rows, columns):
    return jnp.where(rows == columns, 1.0, 0.0).astype(BF16)


def contract(
    order_hbm, bits_hbm, stem_hbm, left_hbm, right_hbm, out,
    order, bits, left, right, stem, product, fy, xh, xl_, gz, gy, bh, bl, y0, w, tt, rr, s3, acc, twin, part, final, last,
    in_sem, z_send, z_recv, x_send, x_recv, base_send, base_recv, y_send, y_recv, d_send, d_recv,
    e_send, e_recv, f_send, f_recv,
    a_send, a_recv, t_send, t_recv, r_send, r_recv, l_send, l_recv,
):
    c, m = lax.axis_index("cuts"), lax.axis_index("mode")
    xl, z = m // 8, lax.rem(m, 8)
    y, xh_, core = c // 4, lax.rem(c // 2, 2), lax.rem(c, 2)
    z_next = [(c, xl * 8 + lax.rem(z + 1, 8)), (c, xl * 8 + lax.rem(z + 7, 8))]
    y_next = [(lax.rem(y + 1, 8) * 4 + lax.rem(c, 4), m), (lax.rem(y + 7, 8) * 4 + lax.rem(c, 4), m)]
    sibling = (c + 1 - 2 * core, m)
    across = (c + 2 - 4 * xh_, m)
    beside = (c, m + 8 - 16 * xl)
    corner = (c + 2 - 4 * xh_, m + 8 - 16 * xl)

    def peer(k):
        return lax.rem(m + k, 16)

    barrier = pltpu.get_barrier_semaphore()

    @pl.loop(1, 16)
    def _(k):
        pl.semaphore_signal(barrier, inc=1, device_id=(c, peer(k)), device_id_type=MESH)

    for target in (*y_next, sibling, across, corner):
        pl.semaphore_signal(barrier, inc=1, device_id=target, device_id_type=MESH)

    loads = [
        pltpu.make_async_copy(src, dst, in_sem.at[n])
        for n, (src, dst) in enumerate(((right_hbm, right), (left_hbm, left), (stem_hbm, stem), (order_hbm, order), (bits_hbm, bits)))
    ]
    for load in loads:
        load.start()

    def remote(src, dst, send, recv, target):
        return pltpu.make_async_remote_copy(
            src_ref=src, dst_ref=dst, send_sem=send, recv_sem=recv, device_id=target, device_id_type=MESH
        )

    def settle(ref, sem):
        pltpu.make_async_copy(ref, ref, sem).wait()

    def go(copy):
        copy.start()

    def multiply():
        loads[0].wait()
        loads[1].wait()
        loads[3].wait()
        loads[4].wait()
        product[...] = dot3(halves(left[...].reshape(384, 512)), halves(right[...]))

    def fragment(t):
        value = product[64 * t : 64 * t + 64]
        first = value.astype(BF16)
        rest = value - first.astype(F32)
        second = rest.astype(BF16)
        third = (rest - second.astype(F32)).astype(BF16)
        stacked = jnp.concatenate([first, second, third], axis=0)
        spot = lax.broadcasted_iota(I32, (8, 512), 1)
        spot = reordered(spot, COLUMNS.get(t, NATURAL9))
        column = jnp.zeros_like(spot)
        for q in range(9):
            bit = jnp.right_shift(spot, jnp.full_like(spot, 8 - order[t, q])) & 1
            column = column + jnp.left_shift(bit, 8 - q)
        moved = dot(stacked, one_hot(lax.broadcasted_iota(I32, (512, 512), 0), column[0:1]))
        pieces = [moved[64 * k : 64 * k + 64] for k in range(3)]
        if t in ROWS:
            new = lax.broadcasted_iota(I32, (64, 64), 0)
            old = (new & 32) + reordered(new & 31, ROWS[t])
            turn = one_hot(lax.broadcasted_iota(I32, (64, 64), 1), old)
            pieces = [dot(turn, p.astype(BF16)) for p in pieces]
        value = pieces[0] + pieces[1] + pieces[2]
        if t in LINE:
            wide = jnp.full((32, 512), bits[0, t], I32)
            gz[m] = jnp.where(wide == 1, value[32:], value[:32])
        else:
            k = RING.index(t)
            for s in range(8):
                for h in range(2):
                    fy[k, s, h] = value[8 * s : 8 * s + 8, 256 * h : 256 * h + 256]
            gy[k, y, core, m] = fy[k, y, core]

    def split_stem():
        loads[2].wait()
        upper = lax.broadcasted_iota(I32, (8, 512), 0) < 4

        @pl.loop(0, 16)
        def _(i):
            for m4 in range(2):
                a = [stem[8 * m4 : 8 * m4 + 8, pl.ds(pl.multiple_of(2048 * i, 2048) + 512 * j, 512)] for j in range(4)]
                low = [jnp.where(upper, a[j], pltpu.roll(a[j + 1], 4, 0)) for j in (0, 2)]
                high = [jnp.where(upper, pltpu.roll(a[j], 4, 0), a[j + 1]) for j in (0, 2)]
                for m5, tiles in enumerate((low, high)):
                    rows = pl.ds(pl.multiple_of(256 * (2 * m4 + m5) + 16 * i, 16), 16)
                    xh[rows], xl_[rows] = halves(jnp.concatenate(tiles, axis=0))

    def x_copy():
        return remote(gz.at[m], gz.at[m], x_send, x_recv, beside)

    def z_copy(cls, d, s):
        owner = lax.rem(z + 8 - (1 - 2 * d) * (s - 1), 8)
        row = (xl * 8 if cls == 0 else (1 - xl) * 8) + owner
        piece = gz.at[row]
        if s == 4:
            piece = gz.at[row, pl.ds(16 * d, 16)]
        return remote(piece, piece, z_send, z_recv.at[cls, d, s - 1], z_next[d])

    def z_first():
        go(x_copy())
        for d in range(2):
            go(z_copy(0, d, 1))

    def z_other():
        x_copy().wait_recv()
        for d in range(2):
            go(z_copy(1, d, 1))

    def z_step(s):
        for cls in range(2):
            for d in range(2):
                z_copy(cls, d, s - 1).wait_recv()
                if s < 5:
                    go(z_copy(cls, d, s))

    def base_copy(g, k):
        pair = pl.ds(*GROUPS[g])
        return remote(
            fy.at[pair, y, core], gy.at[pair, y, core, m],
            base_send, base_recv.at[g], (c, xl * 8 + lax.rem(z + k, 8)),
        )

    def base_start(g):
        @pl.loop(1, 8)
        def _(k):
            base_copy(g, k).start()

    def base_wait(g):
        settle(gy.at[pl.ds(*GROUPS[g]), y, core, pl.ds(0, 7)], base_recv.at[g])

    def y_copy(t, d, s):
        owner = lax.rem(y + 8 - (1 - 2 * d) * (s - 1), 8)
        piece = gy.at[t, owner, core, pl.ds(8 * xl, 8)]
        if s == 4:
            piece = gy.at[t, owner, core, pl.ds(8 * xl + 4 * d, 4)]
        return remote(piece, piece, y_send, y_recv.at[t, d, s - 1], y_next[d])

    def slot(n):
        if n == 0:
            return y
        if n == 7:
            return lax.rem(y + 4, 8)
        return lax.rem(y + 8 - (1 - 2 * ((n - 1) % 2)) * ((n + 1) // 2), 8)

    def d_copy(t, n):
        piece = gy.at[t, slot(n), core, pl.ds(8 * xl, 8)]
        return remote(piece, piece, d_send, d_recv.at[t], sibling)

    def e_copy(t, n, e):
        piece = gy.at[t, slot(n), core, pl.ds(8 * xl + 4 * e, 4)]
        return remote(piece, piece, e_send, e_recv.at[t, n], corner if e else beside)

    def f_copy(t, n):
        piece = gy.at[t, slot(n), core, pl.ds(8 - 8 * xl, 8)]
        return remote(piece, piece, f_send, f_recv.at[t], sibling)

    def share(t, n):
        for e in range(2):
            go(e_copy(t, n, e))
        go(d_copy(t, n))

    def relay(t, n):
        settle(gy.at[t, slot(n), core, pl.ds(8 - 8 * xl, 8)], e_recv.at[t, n])
        go(f_copy(t, n))

    def y_step(t, s):
        if s == 1:
            for g, (first, _) in enumerate(GROUPS):
                if t == first:
                    base_wait(g)
            for d in range(2):
                go(y_copy(t, d, 1))
            share(t, 0)
            return
        for d in range(2):
            y_copy(t, d, s - 1).wait_recv()
            if s < 5:
                go(y_copy(t, d, s))
        if s < 5:
            for d in range(2):
                share(t, 2 * s - 3 + d)
        else:
            share(t, 7)
        for n in (0,) if s == 2 else (2 * s - 5, 2 * s - 4):
            relay(t, n)

    def own_finish(t):
        settle(gy.at[t, :, 1 - core, pl.ds(8 * xl, 8)], d_recv.at[t])

    def other_finish(t):
        settle(gy.at[t, :, 1 - core, pl.ds(8 - 8 * xl, 8)], f_recv.at[t])

    def y_finish(t):
        own_finish(t)
        other_finish(t)

    def prepare_line(k):
        b = LINE[k]

        @pl.loop(0, 4)
        def _(i):
            rows = pl.ds(pl.multiple_of(128 * i, 128), 128)
            bh[b, rows], bl[b, rows] = halves(gz[pl.ds(4 * i, 4)].reshape(128, 512))

    def prepare_ring(t, low=0, count=16):
        b = RING[t]
        one = jnp.full((8, 256), bits[0, b], I32) == 1

        @pl.loop(low, low + count)
        def _(i):
            rows = pl.ds(pl.multiple_of(32 * i, 32), 32)
            for h in range(2):
                lanes = slice(256 * h, 256 * h + 256)
                value = jnp.concatenate(
                    [jnp.where(one, gy[t, 4 + q, h, i], gy[t, q, h, i]) for q in range(4)], axis=0
                )
                bh[b, rows, lanes], bl[b, rows, lanes] = halves(value)

    def prepare_turned(t, turn=None):
        b = RING[t]
        one = jnp.full((1, 8, 256), bits[0, b], I32) == 1

        @pl.loop(0, 4)
        def _(q):
            rows = pl.ds(pl.multiple_of(128 * q, 128), 128)
            for h in range(2):
                lanes = slice(256 * h, 256 * h + 256)
                value = jnp.where(one, gy[t, 4 + q, h], gy[t, q, h]).reshape(128, 256)
                high, low = halves(value)
                if turn is not None:
                    high, low = dot(turn, high).astype(BF16), dot(turn, low).astype(BF16)
                bh[b, rows, lanes], bl[b, rows, lanes] = high, low

    def matrix(b):
        return bh[b], bl[b]

    def absorb0():
        @pl.loop(0, 2)
        def _(i):
            rows = pl.ds(pl.multiple_of(512 * i, 512), 512)
            y0[rows] = dot3((xh[rows], xl_[rows]), matrix(0), True)

    def absorb1():
        @pl.loop(0, 4)
        def _(i):
            rows = pl.ds(pl.multiple_of(256 * i, 256), 256)
            data = jnp.concatenate([y0[rows, :256], y0[rows, 256:]], axis=0)
            w[:, i] = dot3(matrix(1), halves(data)).reshape(4, 128, 256)

    def a_copy(q, target):
        return remote(tt.at[q, target], rr.at[q, m], a_send, a_recv.at[q], (c, target))

    def absorb2(cls, own):
        rows = pl.ds(pl.multiple_of(256 * cls, 256), 256)

        @pl.loop(0, 4)
        def _(q):
            new = dot3((bh[2, rows], bl[2, rows]), halves(w[q].reshape(512, 256)))
            tt[q, pl.ds(8 * cls, 8)] = new.reshape(8, 32, 256)
            if own:
                rr[q, m] = tt[q, m]

            @pl.loop(1 if own else 0, 8)
            def _(k):
                a_copy(q, 8 * cls + lax.rem(z + k, 8)).start()

    def absorb34():
        @pl.loop(0, 2)
        def _(m13):
            @pl.loop(0, 2)
            def _(h):
                q = 2 * m13 + h

                settle(rr.at[q, pl.ds(0, 15)], a_recv.at[q])
                s3[h] = dot3(matrix(3), halves(rr[q].reshape(512, 256)))

            data = jnp.concatenate([s3[0], s3[1]], axis=1)
            new = dot3(halves(data), matrix(4), True)
            for h in range(2):
                w[2 * m13 + h] = new[:, 256 * h : 256 * h + 256].reshape(4, 128, 256)

    def t_copy(i):
        return remote(acc.at[1 - core, i], twin.at[i], t_send, t_recv.at[i], sibling)

    def absorb5(half, low, send):
        rows = pl.ds(pl.multiple_of(256 * half, 256), 256)

        @pl.loop(low, low + 2)
        def _(i):
            data = w[:, i].reshape(512, 256)
            new = dot3((bh[5, rows], bl[5, rows]), halves(data)).reshape(2, 8, 16, 256)
            if send:
                acc[half, i] = new
                t_copy(i).start()
            else:
                t_copy(i).wait_recv()
                acc[half, i] = new + twin[i]

    CHAINS = ((0, 0), (1, 1), (0, 1), (1, 0))

    def steps(k, d):
        return 4 if k == d else 3

    def r_dest(k, d, s):
        return lax.rem(y + 8 + (1 - 2 * d) * (steps(k, d) - s + 1), 8)

    def r_copy(p, k, d, s):
        src = acc.at[core, pl.ds(2 * p, 2), k, r_dest(k, d, s)] if s == 1 else part.at[p, k, d, s - 2]
        return remote(
            src, part.at[p, k, d, s - 1], r_send, r_recv.at[p, k, d, s - 1], y_next[d]
        )

    def r_step(p, s):
        for k, d in CHAINS:
            if s <= steps(k, d):
                if s > 1:
                    r_copy(p, k, d, s - 1).wait_recv()
                    part[p, k, d, s - 2] += acc[core, 2 * p : 2 * p + 2, k, r_dest(k, d, s)]
                go(r_copy(p, k, d, s))

    def l_copy(p):
        return remote(final.at[p, 1 - xh_], last.at[p], l_send, l_recv.at[p], across)

    def r_finish(p):
        for k in range(2):
            for d in range(2):
                r_copy(p, k, d, steps(k, d)).wait_recv()
            total = part[p, k, 0, steps(k, 0) - 1] + part[p, k, 1, steps(k, 1) - 1]
            final[p, k] = acc[core, 2 * p : 2 * p + 2, k, y] + total
        go(l_copy(p))

    def write(p):
        l_copy(p).wait_recv()
        for i in range(2):
            value = final[p, xh_, i] + last[p, i]
            rows = slice(8 * p + 4 * i, 8 * p + 4 * i + 4)
            for n in range(4):
                out[rows, 256 * n : 256 * n + 256] = value[4 * n : 4 * n + 4]

    multiply()
    fragment(0)
    fragment(1)
    pl.semaphore_wait(barrier, 20)
    z_first()
    base_start(0)
    fragment(2)
    fragment(3)
    base_start(1)
    fragment(4)
    fragment(5)
    z_other()
    y_step(0, 1)
    z_step(2)
    y_step(0, 2)
    y_step(1, 1)
    z_step(3)
    y_step(0, 3)
    y_step(1, 2)
    split_stem()
    y_step(0, 4)
    z_step(4)
    base_start(2)
    y_step(1, 3)
    y_step(0, 5)
    z_step(5)
    y_step(1, 4)
    relay(0, 7)
    prepare_line(0)
    absorb0()
    y_step(1, 5)
    y_finish(0)
    prepare_turned(0)
    absorb1()
    own_finish(1)
    prepare_ring(1, 8 * xl, 8)
    absorb2(xl, True)
    relay(1, 7)
    other_finish(1)
    prepare_ring(1, 8 - 8 * xl, 8)
    absorb2(1 - xl, False)
    y_step(2, 1)
    y_step(3, 1)
    y_step(2, 2)
    y_step(3, 2)
    y_step(4, 1)
    y_step(2, 3)
    y_step(3, 3)
    y_step(4, 2)
    y_step(2, 4)
    y_step(3, 4)
    y_step(4, 3)
    y_step(2, 5)
    y_step(3, 5)
    relay(2, 7)
    relay(3, 7)
    y_step(4, 4)
    y_finish(2)
    prepare_ring(2)
    y_step(4, 5)
    y_finish(3)
    prepare_ring(3)
    relay(4, 7)
    y_finish(4)
    new = lax.broadcasted_iota(I32, (128, 128), 0)
    old = reordered(new, (2, 3, 4, 5, 6, 0, 1))
    prepare_turned(4, one_hot(lax.broadcasted_iota(I32, (128, 128), 1), old))
    absorb34()
    for p in range(2):
        absorb5(1 - core, 2 * p, True)
        absorb5(core, 2 * p, False)
        r_step(p, 1)
    for s in range(2, 5):
        for p in range(2):
            r_step(p, s)
    for p in range(2):
        r_finish(p)
    for p in range(2):
        write(p)

    x_copy().wait_send()
    settle(gz.at[pl.ds(0, 14)], z_send)
    settle(fy.at[:, pl.ds(0, 7), 0], base_send)
    settle(gy.at[:, pl.ds(0, 7), 0, pl.ds(0, 8)], y_send)
    for sem in (d_send, e_send, f_send):
        settle(gy.at[:, :, 0, pl.ds(0, 8)], sem)
    settle(tt.at[:, pl.ds(0, 15)], a_send)
    settle(acc.at[0], t_send)
    settle(tt.at[:, pl.ds(0, 7)], r_send)
    settle(last, l_send)


def per_device(stem, left, right, slice_bits, leg_order):
    smem, anywhere = pl.BlockSpec(memory_space=pltpu.SMEM), pl.BlockSpec(memory_space=pl.ANY)
    dma = pltpu.SemaphoreType.DMA
    result = pl.pallas_call(
        contract,
        out_shape=jax.ShapeDtypeStruct((16, 1024), F32),
        in_specs=[anywhere, anywhere, anywhere, anywhere, anywhere],
        out_specs=pl.BlockSpec(memory_space=pltpu.VMEM),
        scratch_shapes=[
            pltpu.SMEM((6, 9), I32),
            pltpu.SMEM((1, 6), I32),
            pltpu.VMEM((6, 2, 32, 512), F32),
            pltpu.VMEM((512, 512), F32),
            pltpu.VMEM((16, 32768), F32),
            pltpu.VMEM((384, 512), F32),
            pltpu.VMEM((5, 8, 2, 8, 256), F32),
            pltpu.VMEM((1024, 512), BF16),
            pltpu.VMEM((1024, 512), BF16),
            pltpu.VMEM((16, 32, 512), F32),
            pltpu.VMEM((5, 8, 2, 16, 8, 256), F32),
            pltpu.VMEM((6, 512, 512), BF16),
            pltpu.VMEM((6, 512, 512), BF16),
            pltpu.VMEM((1024, 512), F32),
            pltpu.VMEM((4, 4, 128, 256), F32),
            pltpu.VMEM((4, 16, 32, 256), F32),
            pltpu.VMEM((4, 16, 32, 256), F32),
            pltpu.VMEM((2, 512, 256), F32),
            pltpu.VMEM((2, 4, 2, 8, 16, 256), F32),
            pltpu.VMEM((4, 2, 8, 16, 256), F32),
            pltpu.VMEM((2, 2, 2, 4, 2, 16, 256), F32),
            pltpu.VMEM((2, 2, 2, 16, 256), F32),
            pltpu.VMEM((2, 2, 16, 256), F32),
            dma((5,)), dma, dma((2, 2, 4)), dma, dma,
            dma, dma((3,)), dma, dma((5, 2, 4)), dma, dma((5,)),
            dma, dma((5, 8)), dma, dma((5,)),
            dma, dma((4,)), dma, dma((4,)),
            dma, dma((2, 2, 2, 4)), dma, dma((2,)),
        ],
        compiler_params=pltpu.CompilerParams(
            collective_id=0, has_side_effects=True, vmem_limit_bytes=56 * 2**20
        ),
    )(leg_order, slice_bits, stem.reshape(16, 32768), left, right)
    return result.reshape(16, 1, 1024)


def solution(mesh):
    in_specs = (
        P("cuts", "mode", None, None),
        P(None, None, "mode", None),
        P(),
        P("cuts", None),
        P(),
    )
    out_specs = P(None, "mode", "cuts")
    return jax.shard_map(per_device, mesh=mesh, in_specs=in_specs, out_specs=out_specs, check_vma=False)
```

```python
import functools

import jax
import jax.numpy as jnp
from jax import lax
from jax.experimental import pallas as pl
from jax.experimental.pallas import tpu as pltpu
from jax.sharding import PartitionSpec as P

F32, BF16, I32 = jnp.float32, jnp.bfloat16, jnp.int32
MESH = pl.DeviceIdType.MESH
LINE = (0,)
RING = (1, 2, 3, 4, 5)
GROUPS = ((0, 1), (1, 2), (3, 2))
NATURAL9 = (0, 1, 2, 3, 4, 5, 6, 7, 8)
COLUMNS = {1: (8, 2, 3, 4, 5, 6, 7, 0, 1), 5: (7, 8, 0, 1, 2, 3, 4, 5, 6)}
ROWS = {1: (3, 4, 0, 1, 2), 5: (2, 1, 0, 3, 4)}


def halves(a):
    high = a.astype(BF16)
    return high, (a - high.astype(F32)).astype(BF16)


def dot(a, b, transposed=False):
    dims = (((1,), (1 if transposed else 0,)), ((), ()))
    return lax.dot_general(a, b, dims, preferred_element_type=F32)


def dot3(a, b, transposed=False):
    (ah, al), (bh, bl) = a, b
    return dot(ah, bl, transposed) + dot(al, bh, transposed) + dot(ah, bh, transposed)


def reordered(index, order):
    bits = len(order)
    total = jnp.zeros_like(index)
    for place, leg in enumerate(order):
        bit = jnp.right_shift(index, bits - 1 - place) & 1
        total = total + jnp.left_shift(bit, bits - 1 - leg)
    return total


def one_hot(rows, columns):
    return jnp.where(rows == columns, 1.0, 0.0).astype(BF16)


def contract(
    order_hbm, bits_hbm, stem_hbm, left_hbm, right_hbm, out,
    order, bits, left, right, stem, product, fy, xh, xl_, gz, gy, bh, bl, y0, w, tt, rr, s3, acc, twin, part, final, last,
    in_sem, z_send, z_recv, x_send, x_recv, base_send, base_recv, y_send, y_recv, d_send, d_recv,
    e_send, e_recv, f_send, f_recv,
    a_send, a_recv, t_send, t_recv, r_send, r_recv, l_send, l_recv,
):
    c, m = lax.axis_index("cuts"), lax.axis_index("mode")
    xl, z = m // 8, lax.rem(m, 8)
    y, xh_, core = c // 4, lax.rem(c // 2, 2), lax.rem(c, 2)
    z_next = [(c, xl * 8 + lax.rem(z + 1, 8)), (c, xl * 8 + lax.rem(z + 7, 8))]
    y_next = [(lax.rem(y + 1, 8) * 4 + lax.rem(c, 4), m), (lax.rem(y + 7, 8) * 4 + lax.rem(c, 4), m)]
    sibling = (c + 1 - 2 * core, m)
    across = (c + 2 - 4 * xh_, m)
    beside = (c, m + 8 - 16 * xl)
    corner = (c + 2 - 4 * xh_, m + 8 - 16 * xl)

    def peer(k):
        return lax.rem(m + k, 16)

    barrier = pltpu.get_barrier_semaphore()

    @pl.loop(1, 16)
    def _(k):
        pl.semaphore_signal(barrier, inc=1, device_id=(c, peer(k)), device_id_type=MESH)

    for target in (*y_next, sibling, across, corner):
        pl.semaphore_signal(barrier, inc=1, device_id=target, device_id_type=MESH)

    loads = [
        pltpu.make_async_copy(src, dst, in_sem.at[n])
        for n, (src, dst) in enumerate(((right_hbm, right), (left_hbm, left), (stem_hbm, stem), (order_hbm, order), (bits_hbm, bits)))
    ]
    for load in loads:
        load.start()

    def remote(src, dst, send, recv, target):
        return pltpu.make_async_remote_copy(
            src_ref=src, dst_ref=dst, send_sem=send, recv_sem=recv, device_id=target, device_id_type=MESH
        )

    def settle(ref, sem):
        pltpu.make_async_copy(ref, ref, sem).wait()

    def go(copy):
        copy.start()

    def multiply():
        loads[0].wait()
        loads[1].wait()
        loads[3].wait()
        loads[4].wait()
        product[...] = dot3(halves(left[...].reshape(384, 512)), halves(right[...]))

    def fragment(t):
        value = product[64 * t : 64 * t + 64]
        first = value.astype(BF16)
        rest = value - first.astype(F32)
        second = rest.astype(BF16)
        third = (rest - second.astype(F32)).astype(BF16)
        stacked = jnp.concatenate([first, second, third], axis=0)
        spot = lax.broadcasted_iota(I32, (8, 512), 1)
        spot = reordered(spot, COLUMNS.get(t, NATURAL9))
        column = jnp.zeros_like(spot)
        for q in range(9):
            bit = jnp.right_shift(spot, jnp.full_like(spot, 8 - order[t, q])) & 1
            column = column + jnp.left_shift(bit, 8 - q)
        moved = dot(stacked, one_hot(lax.broadcasted_iota(I32, (512, 512), 0), column[0:1]))
        pieces = [moved[64 * k : 64 * k + 64] for k in range(3)]
        if t in ROWS:
            new = lax.broadcasted_iota(I32, (64, 64), 0)
            old = (new & 32) + reordered(new & 31, ROWS[t])
            turn = one_hot(lax.broadcasted_iota(I32, (64, 64), 1), old)
            pieces = [dot(turn, p.astype(BF16)) for p in pieces]
        value = pieces[0] + pieces[1] + pieces[2]
        if t in LINE:
            wide = jnp.full((32, 512), bits[0, t], I32)
            gz[m] = jnp.where(wide == 1, value[32:], value[:32])
        else:
            k = RING.index(t)
            for s in range(8):
                for h in range(2):
                    fy[k, s, h] = value[8 * s : 8 * s + 8, 256 * h : 256 * h + 256]
            gy[k, y, core, m] = fy[k, y, core]

    def split_stem():
        loads[2].wait()
        upper = lax.broadcasted_iota(I32, (8, 512), 0) < 4

        @pl.loop(0, 16)
        def _(i):
            for m4 in range(2):
                a = [stem[8 * m4 : 8 * m4 + 8, pl.ds(pl.multiple_of(2048 * i, 2048) + 512 * j, 512)] for j in range(4)]
                low = [jnp.where(upper, a[j], pltpu.roll(a[j + 1], 4, 0)) for j in (0, 2)]
                high = [jnp.where(upper, pltpu.roll(a[j], 4, 0), a[j + 1]) for j in (0, 2)]
                for m5, tiles in enumerate((low, high)):
                    rows = pl.ds(pl.multiple_of(256 * (2 * m4 + m5) + 16 * i, 16), 16)
                    xh[rows], xl_[rows] = halves(jnp.concatenate(tiles, axis=0))

    def x_copy():
        return remote(gz.at[m], gz.at[m], x_send, x_recv, beside)

    def z_copy(cls, d, s):
        owner = lax.rem(z + 8 - (1 - 2 * d) * (s - 1), 8)
        row = (xl * 8 if cls == 0 else (1 - xl) * 8) + owner
        piece = gz.at[row]
        if s == 4:
            piece = gz.at[row, pl.ds(16 * d, 16)]
        return remote(piece, piece, z_send, z_recv.at[cls, d, s - 1], z_next[d])

    def z_first():
        go(x_copy())
        for d in range(2):
            go(z_copy(0, d, 1))

    def z_other():
        x_copy().wait_recv()
        for d in range(2):
            go(z_copy(1, d, 1))

    def z_step(s):
        for cls in range(2):
            for d in range(2):
                z_copy(cls, d, s - 1).wait_recv()
                if s < 5:
                    go(z_copy(cls, d, s))

    def base_copy(g, k):
        pair = pl.ds(*GROUPS[g])
        return remote(
            fy.at[pair, y, core], gy.at[pair, y, core, m],
            base_send, base_recv.at[g], (c, xl * 8 + lax.rem(z + k, 8)),
        )

    def base_start(g):
        @pl.loop(1, 8)
        def _(k):
            base_copy(g, k).start()

    def base_wait(g):
        settle(gy.at[pl.ds(*GROUPS[g]), y, core, pl.ds(0, 7)], base_recv.at[g])

    def y_copy(t, d, s):
        owner = lax.rem(y + 8 - (1 - 2 * d) * (s - 1), 8)
        piece = gy.at[t, owner, core, pl.ds(8 * xl, 8)]
        if s == 4:
            piece = gy.at[t, owner, core, pl.ds(8 * xl + 4 * d, 4)]
        return remote(piece, piece, y_send, y_recv.at[t, d, s - 1], y_next[d])

    def slot(n):
        if n == 0:
            return y
        if n == 7:
            return lax.rem(y + 4, 8)
        return lax.rem(y + 8 - (1 - 2 * ((n - 1) % 2)) * ((n + 1) // 2), 8)

    def d_copy(t, n):
        piece = gy.at[t, slot(n), core, pl.ds(8 * xl, 8)]
        return remote(piece, piece, d_send, d_recv.at[t], sibling)

    def e_copy(t, n, e):
        piece = gy.at[t, slot(n), core, pl.ds(8 * xl + 4 * e, 4)]
        return remote(piece, piece, e_send, e_recv.at[t, n], corner if e else beside)

    def f_copy(t, n):
        piece = gy.at[t, slot(n), core, pl.ds(8 - 8 * xl, 8)]
        return remote(piece, piece, f_send, f_recv.at[t], sibling)

    def share(t, n):
        for e in range(2):
            go(e_copy(t, n, e))
        go(d_copy(t, n))

    def relay(t, n):
        settle(gy.at[t, slot(n), core, pl.ds(8 - 8 * xl, 8)], e_recv.at[t, n])
        go(f_copy(t, n))

    def y_step(t, s):
        if s == 1:
            for g, (first, _) in enumerate(GROUPS):
                if t == first:
                    base_wait(g)
            for d in range(2):
                go(y_copy(t, d, 1))
            share(t, 0)
            return
        for d in range(2):
            y_copy(t, d, s - 1).wait_recv()
            if s < 5:
                go(y_copy(t, d, s))
        if s < 5:
            for d in range(2):
                share(t, 2 * s - 3 + d)
        else:
            share(t, 7)
        for n in (0,) if s == 2 else (2 * s - 5, 2 * s - 4):
            relay(t, n)

    def own_finish(t):
        settle(gy.at[t, :, 1 - core, pl.ds(8 * xl, 8)], d_recv.at[t])

    def other_finish(t):
        settle(gy.at[t, :, 1 - core, pl.ds(8 - 8 * xl, 8)], f_recv.at[t])

    def y_finish(t):
        own_finish(t)
        other_finish(t)

    def prepare_line(k):
        b = LINE[k]

        @pl.loop(0, 4)
        def _(i):
            rows = pl.ds(pl.multiple_of(128 * i, 128), 128)
            bh[b, rows], bl[b, rows] = halves(gz[pl.ds(4 * i, 4)].reshape(128, 512))

    def prepare_ring(t, low=0, count=16):
        b = RING[t]
        one = jnp.full((8, 256), bits[0, b], I32) == 1

        @pl.loop(low, low + count)
        def _(i):
            rows = pl.ds(pl.multiple_of(32 * i, 32), 32)
            for h in range(2):
                lanes = slice(256 * h, 256 * h + 256)
                value = jnp.concatenate(
                    [jnp.where(one, gy[t, 4 + q, h, i], gy[t, q, h, i]) for q in range(4)], axis=0
                )
                bh[b, rows, lanes], bl[b, rows, lanes] = halves(value)

    def prepare_turned(t, turn=None):
        b = RING[t]
        one = jnp.full((1, 8, 256), bits[0, b], I32) == 1

        @pl.loop(0, 4)
        def _(q):
            rows = pl.ds(pl.multiple_of(128 * q, 128), 128)
            for h in range(2):
                lanes = slice(256 * h, 256 * h + 256)
                value = jnp.where(one, gy[t, 4 + q, h], gy[t, q, h]).reshape(128, 256)
                high, low = halves(value)
                if turn is not None:
                    high, low = dot(turn, high).astype(BF16), dot(turn, low).astype(BF16)
                bh[b, rows, lanes], bl[b, rows, lanes] = high, low

    def matrix(b):
        return bh[b], bl[b]

    def absorb0():
        @pl.loop(0, 2)
        def _(i):
            rows = pl.ds(pl.multiple_of(512 * i, 512), 512)
            y0[rows] = dot3((xh[rows], xl_[rows]), matrix(0), True)

    def absorb1():
        @pl.loop(0, 4)
        def _(i):
            rows = pl.ds(pl.multiple_of(256 * i, 256), 256)
            data = jnp.concatenate([y0[rows, :256], y0[rows, 256:]], axis=0)
            w[:, i] = dot3(matrix(1), halves(data)).reshape(4, 128, 256)

    def a_copy(q, target):
        return remote(tt.at[q, target], rr.at[q, m], a_send, a_recv.at[q], (c, target))

    def absorb2(cls, own):
        rows = pl.ds(pl.multiple_of(256 * cls, 256), 256)

        @pl.loop(0, 4)
        def _(q):
            new = dot3((bh[2, rows], bl[2, rows]), halves(w[q].reshape(512, 256)))
            tt[q, pl.ds(8 * cls, 8)] = new.reshape(8, 32, 256)
            if own:
                rr[q, m] = tt[q, m]

            @pl.loop(1 if own else 0, 8)
            def _(k):
                a_copy(q, 8 * cls + lax.rem(z + k, 8)).start()

    def absorb34():
        @pl.loop(0, 2)
        def _(m13):
            @pl.loop(0, 2)
            def _(h):
                q = 2 * m13 + h

                settle(rr.at[q, pl.ds(0, 15)], a_recv.at[q])
                s3[h] = dot3(matrix(3), halves(rr[q].reshape(512, 256)))

            data = jnp.concatenate([s3[0], s3[1]], axis=1)
            new = dot3(halves(data), matrix(4), True)
            for h in range(2):
                w[2 * m13 + h] = new[:, 256 * h : 256 * h + 256].reshape(4, 128, 256)

    def t_copy(i):
        return remote(acc.at[1 - core, i], twin.at[i], t_send, t_recv.at[i], sibling)

    def absorb5(half, low, send):
        rows = pl.ds(pl.multiple_of(256 * half, 256), 256)

        @pl.loop(low, low + 2)
        def _(i):
            data = w[:, i].reshape(512, 256)
            new = dot3((bh[5, rows], bl[5, rows]), halves(data)).reshape(2, 8, 16, 256)
            if send:
                acc[half, i] = new
                t_copy(i).start()
            else:
                t_copy(i).wait_recv()
                acc[half, i] = new + twin[i]

    CHAINS = ((0, 0), (1, 1), (0, 1), (1, 0))

    def steps(k, d):
        return 4 if k == d else 3

    def r_dest(k, d, s):
        return lax.rem(y + 8 + (1 - 2 * d) * (steps(k, d) - s + 1), 8)

    def r_copy(p, k, d, s):
        src = acc.at[core, pl.ds(2 * p, 2), k, r_dest(k, d, s)] if s == 1 else part.at[p, k, d, s - 2]
        return remote(
            src, part.at[p, k, d, s - 1], r_send, r_recv.at[p, k, d, s - 1], y_next[d]
        )

    def r_step(p, s):
        for k, d in CHAINS:
            if s <= steps(k, d):
                if s > 1:
                    r_copy(p, k, d, s - 1).wait_recv()
                    part[p, k, d, s - 2] += acc[core, 2 * p : 2 * p + 2, k, r_dest(k, d, s)]
                go(r_copy(p, k, d, s))

    def l_copy(p):
        return remote(final.at[p, 1 - xh_], last.at[p], l_send, l_recv.at[p], across)

    def r_finish(p):
        for k in range(2):
            for d in range(2):
                r_copy(p, k, d, steps(k, d)).wait_recv()
            total = part[p, k, 0, steps(k, 0) - 1] + part[p, k, 1, steps(k, 1) - 1]
            final[p, k] = acc[core, 2 * p : 2 * p + 2, k, y] + total
        go(l_copy(p))

    def write(p):
        l_copy(p).wait_recv()
        for i in range(2):
            value = final[p, xh_, i] + last[p, i]
            rows = slice(8 * p + 4 * i, 8 * p + 4 * i + 4)
            for n in range(4):
                out[rows, 256 * n : 256 * n + 256] = value[4 * n : 4 * n + 4]

    multiply()
    fragment(0)
    fragment(1)
    pl.semaphore_wait(barrier, 20)
    z_first()
    base_start(0)
    fragment(2)
    fragment(3)
    base_start(1)
    fragment(4)
    fragment(5)
    z_other()
    y_step(0, 1)
    z_step(2)
    y_step(0, 2)
    y_step(1, 1)
    z_step(3)
    y_step(0, 3)
    y_step(1, 2)
    split_stem()
    y_step(0, 4)
    z_step(4)
    base_start(2)
    y_step(1, 3)
    y_step(0, 5)
    z_step(5)
    y_step(1, 4)
    prepare_line(0)
    relay(0, 7)
    absorb0()
    y_step(1, 5)
    y_finish(0)
    prepare_turned(0)
    absorb1()
    own_finish(1)
    prepare_ring(1, 8 * xl, 8)
    absorb2(xl, True)
    relay(1, 7)
    other_finish(1)
    prepare_ring(1, 8 - 8 * xl, 8)
    absorb2(1 - xl, False)
    y_step(2, 1)
    y_step(3, 1)
    y_step(2, 2)
    y_step(3, 2)
    y_step(4, 1)
    y_step(2, 3)
    y_step(3, 3)
    y_step(4, 2)
    y_step(2, 4)
    y_step(3, 4)
    y_step(4, 3)
    y_step(2, 5)
    y_step(3, 5)
    relay(2, 7)
    relay(3, 7)
    y_step(4, 4)
    y_finish(2)
    prepare_ring(2)
    y_step(4, 5)
    y_finish(3)
    prepare_ring(3)
    relay(4, 7)
    y_finish(4)
    new = lax.broadcasted_iota(I32, (128, 128), 0)
    old = reordered(new, (2, 3, 4, 5, 6, 0, 1))
    prepare_turned(4, one_hot(lax.broadcasted_iota(I32, (128, 128), 1), old))
    absorb34()
    for p in range(2):
        absorb5(1 - core, 2 * p, True)
        absorb5(core, 2 * p, False)
        r_step(p, 1)
    for s in range(2, 5):
        for p in range(2):
            r_step(p, s)
    for p in range(2):
        r_finish(p)
    for p in range(2):
        write(p)

    x_copy().wait_send()
    settle(gz.at[pl.ds(0, 14)], z_send)
    settle(fy.at[:, pl.ds(0, 7), 0], base_send)
    settle(gy.at[:, pl.ds(0, 7), 0, pl.ds(0, 8)], y_send)
    for sem in (d_send, e_send, f_send):
        settle(gy.at[:, :, 0, pl.ds(0, 8)], sem)
    settle(tt.at[:, pl.ds(0, 15)], a_send)
    settle(acc.at[0], t_send)
    settle(tt.at[:, pl.ds(0, 7)], r_send)
    settle(last, l_send)


def per_device(stem, left, right, slice_bits, leg_order):
    smem, anywhere = pl.BlockSpec(memory_space=pltpu.SMEM), pl.BlockSpec(memory_space=pl.ANY)
    dma = pltpu.SemaphoreType.DMA
    result = pl.pallas_call(
        contract,
        out_shape=jax.ShapeDtypeStruct((16, 1024), F32),
        in_specs=[anywhere, anywhere, anywhere, anywhere, anywhere],
        out_specs=pl.BlockSpec(memory_space=pltpu.VMEM),
        scratch_shapes=[
            pltpu.SMEM((6, 9), I32),
            pltpu.SMEM((1, 6), I32),
            pltpu.VMEM((6, 2, 32, 512), F32),
            pltpu.VMEM((512, 512), F32),
            pltpu.VMEM((16, 32768), F32),
            pltpu.VMEM((384, 512), F32),
            pltpu.VMEM((5, 8, 2, 8, 256), F32),
            pltpu.VMEM((1024, 512), BF16),
            pltpu.VMEM((1024, 512), BF16),
            pltpu.VMEM((16, 32, 512), F32),
            pltpu.VMEM((5, 8, 2, 16, 8, 256), F32),
            pltpu.VMEM((6, 512, 512), BF16),
            pltpu.VMEM((6, 512, 512), BF16),
            pltpu.VMEM((1024, 512), F32),
            pltpu.VMEM((4, 4, 128, 256), F32),
            pltpu.VMEM((4, 16, 32, 256), F32),
            pltpu.VMEM((4, 16, 32, 256), F32),
            pltpu.VMEM((2, 512, 256), F32),
            pltpu.VMEM((2, 4, 2, 8, 16, 256), F32),
            pltpu.VMEM((4, 2, 8, 16, 256), F32),
            pltpu.VMEM((2, 2, 2, 4, 2, 16, 256), F32),
            pltpu.VMEM((2, 2, 2, 16, 256), F32),
            pltpu.VMEM((2, 2, 16, 256), F32),
            dma((5,)), dma, dma((2, 2, 4)), dma, dma,
            dma, dma((3,)), dma, dma((5, 2, 4)), dma, dma((5,)),
            dma, dma((5, 8)), dma, dma((5,)),
            dma, dma((4,)), dma, dma((4,)),
            dma, dma((2, 2, 2, 4)), dma, dma((2,)),
        ],
        compiler_params=pltpu.CompilerParams(
            collective_id=0, has_side_effects=True, vmem_limit_bytes=56 * 2**20
        ),
    )(leg_order, slice_bits, stem.reshape(16, 32768), left, right)
    return result.reshape(16, 1, 1024)


def solution(mesh):
    in_specs = (
        P("cuts", "mode", None, None),
        P(None, None, "mode", None),
        P(),
        P("cuts", None),
        P(),
    )
    out_specs = P(None, "mode", "cuts")
    return jax.shard_map(per_device, mesh=mesh, in_specs=in_specs, out_specs=out_specs, check_vma=False)
```
